32 devices in a mesh: groups: 2 (over y), tile: 16 (over z, x, core).
Axes of the slice: x: 2, y: 2, z: 4, core: 2. Of those that a mesh axis runs over, the one named last changes fastest.
Arguments:
- rhs: float32 [4096, 320], P(('groups', 'tile')), parts along dimension 0, may hold values from -8 to 8
- counts: int32 [32], P('groups'), parts along dimension 0, may hold values from 32 to 128, as said below
- local_target: int32 [4096, 24], P(('groups', 'tile')), parts along dimension 0, may hold values from 0 to 127
- local_offset: int32 [4096, 24], P(('groups', 'tile')), parts along dimension 0, may hold values from 0 to 31
- remote_tile: int32 [4096, 4], P(('groups', 'tile')), parts along dimension 0, may hold values from 0 to 15, all different within a row; in each aligned block of 128 rows (0 to 127, 128 to 255, ...) at most 64 rows name the same one
- remote_target: int32 [4096, 4], P(('groups', 'tile')), parts along dimension 0, may hold values from 0 to 127
- remote_offset: int32 [4096, 4], P(('groups', 'tile')), parts along dimension 0, may hold values from 0 to 31
- lattice: bfloat16 [32, 320, 320], replicated, may hold values from -2 to 2
- tmatrix: bfloat16 [320, 320], replicated, may hold values from -1 to 1
Outputs:
- basis: float32 [4, 4096, 320], P(None, ('groups', 'tile')), parts along dimension 1
- hess: float32 [8, 3], P('groups'), parts along dimension 0
The draws below stay inside these ranges and needn't reach their ends.
There are 2 independent parts, one for each index of `groups`. The reference program is written for one: setup_inputs(seed, part) draws one part's arguments, and reference() takes and returns one part's arrays. A program takes and returns all parts, laid end to end along the dimension named above; an argument that names none is the same for every part. Nothing has to cross between parts.
Inputs may be any that keep to these rules, and one draw needn't show every extreme that they name: counts[t] is a tile's live clusters; some tile has all 128 slots live. `remote_tile`: each cluster names 4 different tiles; among the clusters of one tile, no tile is named more than 64 times.
All inputs are finite; a program needn't handle non-finite values.
Results may differ from the reference program's by a relative error of at most 0.0048.
Values may be sent and summed in bfloat16 or wider, within the bound.
No kernel may reach another device: no remote copies, remote signals or barrier semaphores. Data moves between devices by JAX's collectives and lax.ppermute only.
A program may use at most 64 MiB of HBM per device.

```python
import math
import jax
import jax.numpy as jnp
import numpy as np
from jax import lax

K = 320
NOFF = 32
NL = 24
NR = 4
CAP = 128
ITERS = 3
SEND_CAP = 64
CLUSTERS = 2048
N_TILE = 16


def draw_counts(key, part):
    key = jax.random.fold_in(key, 7)
    first, second = jax.random.split(key)
    values = jax.random.randint(first, (N_TILE,), CAP // 4, CAP + 1).astype(jnp.int32)
    where_full = jax.random.randint(second, (), 0, N_TILE)
    return values.at[where_full].set(CAP).astype(jnp.int32)


def symmetric_noise(key, shape):
    values = jnp.clip(jax.random.normal(key, shape, jnp.float32), -5.0, 5.0)
    return (values + jnp.swapaxes(values, -1, -2)) / math.sqrt(2.0)


def draw_rhs(key, part):
    key = jax.random.fold_in(key, 13)
    first, second, third = jax.random.split(key, 3)
    common = jax.random.normal(first, (1, K), jnp.float32)
    noise = jax.random.normal(second, (CLUSTERS, K), jnp.float32)
    amplitude = jnp.exp(jax.random.uniform(third, (CLUSTERS, 1), jnp.float32, math.log(0.7), math.log(1.4)))
    return jnp.clip(amplitude * common + 0.5 * noise, -8.0, 8.0).astype(jnp.float32)


def draw_lattice(key, part):
    key = jax.random.fold_in(key, 17)
    first, second, third = jax.random.split(key, 3)
    shared = symmetric_noise(first, (K, K))
    own = symmetric_noise(second, (NOFF, K, K))
    diagonal = 0.5 * jax.random.uniform(third, (NOFF, K), jnp.float32, 0.7, 1.3)
    spread = 0.6 / math.sqrt(K)
    eye = jnp.eye(K, dtype=jnp.float32)
    values = diagonal[:, :, None] * eye[None, :, :] + spread * (shared[None, :, :] + own)
    return jnp.clip(values, -2.0, 2.0).astype(jnp.bfloat16)


def draw_tmatrix(key, part):
    key = jax.random.fold_in(key, 19)
    first, second = jax.random.split(key)
    level = 0.6 / (NL + NR)
    noise = symmetric_noise(first, (K, K))
    diagonal = level * jax.random.uniform(second, (K,), jnp.float32, 0.7, 1.3)
    values = jnp.diag(diagonal) + 0.3 * level / math.sqrt(K) * noise
    return jnp.clip(values, -1.0, 1.0).astype(jnp.bfloat16)


def set_ends(drawn, key, smallest, top_value):
    place = [jax.random.randint(jax.random.fold_in(key, axis), (), 0, length) for axis, length in enumerate(drawn.shape)]
    longest = drawn.shape.index(max(drawn.shape))
    next_to = place[:longest] + [(place[longest] + 1) % drawn.shape[longest]] + place[longest + 1:]
    return drawn.at[tuple(place)].set(smallest).at[tuple(next_to)].set(top_value)


def assign_block(stream_key, own, number, rows, amount, top, limit, slope):
    sequence = jax.random.permutation(stream_key, amount)
    crowded, usual = portions_of(amount, rows * top, limit, slope, True), portions_of(amount, rows * top, limit, slope, False)
    places = jnp.arange(amount)

    def named(lengths, turn):
        used = int((lengths > 0).sum())
        fixed = max(1, used // 4)
        shifted = fixed + (places - fixed + turn * (used - fixed)) % max(1, amount - fixed)
        return jnp.zeros((amount,), jnp.int32).at[sequence[jnp.where(places < fixed, places, shifted)]].set(jnp.asarray(lengths, jnp.int32))

    lengths = jnp.where(number % 4 == 0, named(crowded, number // 4), named(usual, number - number // 4 - 1))
    mixed = jax.random.permutation(jax.random.fold_in(own, 3), amount)
    source_of, sink = mixed[0:amount // 2 * 2:2], mixed[1:amount // 2 * 2:2]
    room = jnp.minimum(lengths[source_of] - 1, limit - lengths[sink]) // 2
    room = jnp.where((source_of == sequence[0]) | (sink == sequence[0]) | (lengths[sink] == 0), 0, jnp.maximum(room, 0))
    shifted = jax.random.randint(jax.random.fold_in(own, 4), (amount // 2,), 0, 1 << 20) % (room + 1)
    lengths = lengths.at[source_of].add(-shifted).at[sink].add(shifted)
    labels = jnp.searchsorted(jnp.cumsum(lengths), jnp.arange(rows * top), side="right").astype(jnp.int32)
    grid = labels.reshape(top, rows).T
    grid = grid[jax.random.permutation(jax.random.fold_in(own, 1), rows)]
    turn = jax.random.randint(jax.random.fold_in(own, 2), (rows, 1), 0, top)
    return jnp.take_along_axis(grid, (jnp.arange(top)[None, :] + turn) % top, axis=1)


def portions_of(amount, total, reach, skew, full):
    loads = [(1 << 20) // math.isqrt(grade ** skew) + 1 for grade in range(1, amount + 1)]
    largest = reach if full else min(reach, max(-(-total // amount), total * loads[0] // sum(loads)))
    least = 1 if total - largest >= amount - 1 else 0
    holding, spare = [largest] + [least] * (amount - 1), total - largest - least * (amount - 1)
    while spare > 0:
        free = [i for i in range(1, amount) if holding[i] < largest] or [i for i in range(1, amount) if holding[i] < reach]
        mass, remaining = sum([loads[i] for i in free]), spare
        for i in free:
            addition = min(reach - holding[i], max(1, remaining * loads[i] // mass), spare)
            holding[i] = holding[i] + addition
            spare = spare - addition
    return np.array(holding)


def setup_inputs(seed: int = 0, part: int = 0) -> dict:
    key_list = jax.random.split(jax.random.key(seed), 10)
    part_splits = jax.random.split(jax.random.fold_in(key_list[9], part), 10)
    rhs = draw_rhs(jax.random.fold_in(jax.random.fold_in(key_list[9], part), 71), part)
    counts = draw_counts(jax.random.fold_in(jax.random.fold_in(key_list[9], part), 71), part)
    local_target = set_ends(jax.random.randint(part_splits[2], (CLUSTERS, NL), 0, CAP), jax.random.fold_in(part_splits[2], 1), 0, CAP - 1).astype(jnp.int32)
    local_offset = set_ends(jax.random.randint(part_splits[3], (CLUSTERS, NL), 0, NOFF), jax.random.fold_in(part_splits[3], 1), 0, NOFF - 1).astype(jnp.int32)
    remote_tile_keys = jax.random.split(jax.random.fold_in(part_splits[4], 1), CLUSTERS // CAP)
    remote_tile_turns = jax.random.permutation(jax.random.fold_in(part_splits[4], 3), CLUSTERS // CAP)
    remote_tile = jax.vmap(lambda own, number: assign_block(jax.random.fold_in(part_splits[4], 2), own, number, CAP, N_TILE, NR, SEND_CAP, 2))(remote_tile_keys, remote_tile_turns).reshape((CLUSTERS, NR))
    remote_target = set_ends(jax.random.randint(part_splits[5], (CLUSTERS, NR), 0, CAP), jax.random.fold_in(part_splits[5], 1), 0, CAP - 1).astype(jnp.int32)
    remote_offset = set_ends(jax.random.randint(part_splits[6], (CLUSTERS, NR), 0, NOFF), jax.random.fold_in(part_splits[6], 1), 0, NOFF - 1).astype(jnp.int32)
    lattice = draw_lattice(jax.random.fold_in(key_list[9], 71), part)
    tmatrix = draw_tmatrix(jax.random.fold_in(key_list[9], 71), part)
    return dict(rhs=rhs, counts=counts, local_target=local_target, local_offset=local_offset, remote_tile=remote_tile, remote_target=remote_target, remote_offset=remote_offset, lattice=lattice, tmatrix=tmatrix)


def reference(rhs, counts, local_target, local_offset, remote_tile, remote_target, remote_offset, lattice, tmatrix):
    index_all = jnp.arange(CLUSTERS, dtype=jnp.int32)
    tile_of = index_all // CAP
    slot_of = index_all % CAP
    live = (slot_of < counts[tile_of]).astype(jnp.float32)
    start = rhs * live[:, None]
    dump = CAP * NOFF
    local_code = (local_target % counts[tile_of][:, None] * NOFF + local_offset).reshape(-1).astype(jnp.int32)
    remote_dest = remote_tile.reshape(-1).astype(jnp.int32)
    remote_code = (remote_target % counts[remote_tile] * NOFF + remote_offset).reshape(-1).astype(jnp.int32)
    remote_src = (jnp.arange(CLUSTERS * NR, dtype=jnp.int32) // NR).astype(jnp.int32)
    order = jnp.argsort(remote_dest, stable=True).astype(jnp.int32)
    window = N_TILE * SEND_CAP
    sorted_src = jnp.concatenate([remote_src[order], jnp.zeros((window,), jnp.int32)])
    sorted_code = jnp.concatenate([remote_code[order], jnp.full((window,), dump, jnp.int32)])
    sorted_dest = jnp.concatenate([remote_dest[order], jnp.full((window,), -1, jnp.int32)])
    incoming = lax.optimization_barrier(jnp.sum((remote_dest[:, None] == jnp.arange(N_TILE, dtype=jnp.int32)[None, :]).astype(jnp.int32), axis=0))
    starts = (jnp.cumsum(incoming) - incoming).astype(jnp.int32)
    lattice_flat = lattice.reshape(NOFF * K, K)

    def operate(vector):
        xb = vector.astype(jnp.bfloat16)

        def per_tile(tile):
            begin = starts[tile]
            src = lax.dynamic_slice_in_dim(sorted_src, begin, window, 0)
            code = lax.dynamic_slice_in_dim(sorted_code, begin, window, 0)
            dest = lax.dynamic_slice_in_dim(sorted_dest, begin, window, 0)
            code = jnp.where(dest == tile, code, dump).astype(jnp.int32)
            own_rows = lax.dynamic_slice_in_dim(xb, (tile * CAP).astype(jnp.int32), CAP, 0)
            own_codes = lax.dynamic_slice_in_dim(local_code, (tile * CAP * NL).astype(jnp.int32), CAP * NL, 0)
            rows = jnp.concatenate([jnp.repeat(own_rows, NL, axis=0), xb[src]]).astype(jnp.float32)
            codes = jnp.concatenate([own_codes, code])
            summed = jax.ops.segment_sum(rows, codes, num_segments=dump + 1)
            summed = summed[:dump].reshape(CAP, NOFF * K).astype(jnp.bfloat16)
            field = jnp.dot(summed, lattice_flat, preferred_element_type=jnp.float32).astype(jnp.bfloat16)
            return jnp.dot(field, tmatrix, preferred_element_type=jnp.float32)
        scattered = lax.map(per_tile, jnp.arange(N_TILE, dtype=jnp.int32)).reshape(CLUSTERS, K)
        return vector - live[:, None] * scattered
    beta = jnp.sqrt(jnp.sum(start * start))
    vectors = [start / beta]
    hess = jnp.zeros((ITERS + 1, ITERS), jnp.float32)
    for step in range(ITERS):
        image = operate(vectors[step])
        products = [jnp.sum(vectors[j] * image) for j in range(step + 1)]
        for j in range(step + 1):
            image = image - products[j] * vectors[j]
            hess = hess.at[j, step].set(products[j])
        length = jnp.sqrt(jnp.sum(image * image))
        hess = hess.at[step + 1, step].set(length)
        vectors.append(image / length)
    return (jnp.stack(vectors), hess)
```

```python
import functools

import jax
import jax.numpy as jnp
from jax import lax
from jax.experimental import pallas as pl
from jax.experimental.pallas import tpu as pltpu
from jax.sharding import PartitionSpec as P

ITERS = 3
LANES = 128
GROUP = 4
F32 = jnp.float32
BF16 = jnp.bfloat16
VMEM_LIMIT = 56 * 1024 * 1024


def iota(shape, dim):
    return lax.broadcasted_iota(jnp.int32, shape, dim)


def dot(a, b):
    return lax.dot_general(a, b, (((1,), (0,)), ((), ())), preferred_element_type=F32)


def dot_nt(a, b):
    return lax.dot_general(a, b, (((1,), (1,)), ((), ())), preferred_element_type=F32)


def flip(table):
    rows = table.shape[0]
    eye = (iota((rows, rows), 0) == iota((rows, rows), 1)).astype(BF16)
    return lax.dot_general(
        table.astype(F32).astype(BF16), eye, (((0,), (0,)), ((), ())), preferred_element_type=F32
    )


def total(values):
    return jnp.sum(jnp.sum(values, axis=0, keepdims=True), axis=1, keepdims=True)


def pieces(value):
    first = value.astype(BF16).astype(F32)
    rest = value - first
    second = rest.astype(BF16).astype(F32)
    return first, second, (rest - second)


def wrap(target, count):
    for _ in range(3):
        target = jnp.where(target >= count, target - count, target)
    return target


class Shape:
    def __init__(self, tiles, cap, width, nl, nr, noff):
        self.tiles, self.cap, self.width, self.nl, self.nr, self.noff = tiles, cap, width, nl, nr, noff
        self.send_cap = max(2, 2 * cap * nr // tiles)
        self.slots = max(16, self.send_cap)
        self.fold = 2 if self.slots % 32 == 0 else 1
        self.full = width // LANES
        self.rest = width - self.full * LANES
        self.tail = self.slots // self.fold
        self.head = self.full * self.slots
        self.extra = self.head + self.tail
        self.rows = self.extra + 16
        self.per = LANES // self.slots
        self.chunks = tiles // self.per
        self.inbound = tiles * self.slots


def pack(sh, values, rank_ref, out_ref, sel_ref):
    for d in range(sh.tiles):
        picked = (rank_ref[d : d + 1, :] == iota((sh.slots, sh.cap), 0)).astype(F32).astype(BF16)
        sel_ref[d * sh.slots : (d + 1) * sh.slots, :] = picked
    rows = dot(sel_ref[...], values).astype(BF16)
    for d in range(sh.tiles):
        block = rows[d * sh.slots : (d + 1) * sh.slots]
        for p in range(sh.full):
            out_ref[d, p * sh.slots : (p + 1) * sh.slots, :] = block[:, p * LANES : (p + 1) * LANES]
        last = block[:, sh.full * LANES :]
        if sh.fold == 2:
            last = jnp.concatenate([last[: sh.tail], last[sh.tail :]], axis=1)
        else:
            last = jnp.concatenate([last, jnp.zeros_like(last)], axis=1)
        out_ref[d, sh.head : sh.extra, :] = last


def sum_rows(sums):
    row = iota((16, LANES), 0)
    tile = jnp.zeros((16, LANES), F32)
    for q, value in enumerate(sums):
        for p, piece in enumerate(pieces(value)):
            tile = jnp.where(row == 4 + 3 * q + p, piece, tile)
    return tile


def first_kernel(sh, mine_ref, counts_ref, rhs_ref, tile_ref, target_ref, offset_ref,
                 start_ref, rank_out, out_ref, sel_ref, rank_ref):
    mine = mine_ref[0]
    count = counts_ref[mine]
    live = (iota((sh.cap, 1), 0) < count).astype(F32)
    start = rhs_ref[...] * live
    start_ref[...] = start
    tile = flip(tile_ref[...]).astype(jnp.int32)
    target = flip(target_ref[...])
    offset = flip(offset_ref[...])
    which = iota((sh.tiles, sh.cap), 0)
    named = jnp.zeros((sh.tiles, sh.cap), F32)
    targets = jnp.zeros((sh.tiles, sh.cap), F32)
    offsets = jnp.zeros((sh.tiles, sh.cap), F32)
    for r in range(sh.nr):
        hit = tile[r : r + 1, :] == which
        named = jnp.where(hit, 1.0, named)
        targets = jnp.where(hit, target[r : r + 1, :], targets)
        offsets = jnp.where(hit, offset[r : r + 1, :], offsets)
    before = (iota((sh.cap, sh.cap), 0) < iota((sh.cap, sh.cap), 1)).astype(F32).astype(BF16)
    rank = dot(named.astype(BF16), before).astype(jnp.int32)
    rank = jnp.where(named > 0.0, rank, -LANES)
    rank_ref[...] = rank
    rank_out[...] = rank
    pack(sh, start.astype(BF16), rank_ref, out_ref, sel_ref)
    sums = sum_rows([total(start * start)])
    shift = lax.rem(mine, sh.per) * sh.slots
    row = iota((16, LANES), 0)
    for d in range(sh.tiles):
        picked = (rank[d : d + 1, :] + shift == iota((LANES, sh.cap), 0)).astype(F32).astype(BF16)
        table = jnp.where(row == 0, targets[d : d + 1, :], 0.0)
        table = jnp.where(row == 1, offsets[d : d + 1, :], table)
        table = jnp.where(row == 2, named[d : d + 1, :], table)
        extra = dot_nt(table.astype(BF16), picked) + sums
        out_ref[d, sh.extra :, :] = extra.astype(BF16)


def local_kernel(sh, mine_ref, counts_ref, target_ref, offset_ref, pairs_ref, code_ref):
    count = counts_ref[mine_ref[0]]
    target = wrap(flip(target_ref[...]).astype(jnp.int32), count)
    code_ref[...] = target * sh.noff + flip(offset_ref[...]).astype(jnp.int32)

    def body(o, carry):
        mark = iota((sh.cap, sh.cap), 0) * sh.noff + o
        amount = jnp.zeros((sh.cap, sh.cap), F32)
        for n in range(sh.nl):
            amount = amount + (code_ref[n : n + 1, :] == mark).astype(F32)
        pairs_ref[o] = amount.astype(BF16)
        return carry

    lax.fori_loop(0, sh.noff, body, 0)


def next_vector(step, current, olds, sums):
    if step == 0:
        return current / jnp.sqrt(sums[0])
    square = sums[step]
    kept = current
    for j in range(step):
        square = square - sums[j] * sums[j]
        kept = kept - sums[j] * olds[j]
    return -kept / jnp.sqrt(square)


def step_kernel(sh, step, *refs):
    refs = list(refs)
    take = lambda n: [refs.pop(0) for _ in range(n)]
    mine_ref, counts_ref, recv_ref, rank_ref, pairs_ref, tmatrix_ref, lattice_ref, current_ref = take(8)
    olds = take(step)
    copies = take(step)
    code_in = take(1 if step else 0)
    vector_out, image_out, sums_out = take(3)
    last = step == ITERS - 1
    send_out = take(1)[0]
    copy_out = None if last else take(1)[0]
    code_out = take(0 if step else 1)
    lattice_vmem, sems, x_ref, p_ref, sel_ref = refs
    groups = sh.noff // GROUP
    loads = [
        pltpu.make_async_copy(
            lattice_ref.at[pl.ds(g * GROUP, GROUP)], lattice_vmem.at[pl.ds(g * GROUP, GROUP)], sems.at[g]
        )
        for g in range(groups)
    ]
    for load in loads:
        load.start()
    count = counts_ref[mine_ref[0]]
    extras = jnp.zeros((16, LANES), F32)
    for s in range(sh.tiles):
        extras = extras + recv_ref[s, sh.extra :, :].astype(F32)
    sums = []
    for q in range(max(1, step + 1)):
        r = 4 + 3 * q
        three = extras[r : r + 1, 0:1] + extras[r + 1 : r + 2, 0:1] + extras[r + 2 : r + 3, 0:1]
        sums.append(three)
    vector = next_vector(step, current_ref[...], [ref[...] for ref in olds], sums)
    vector_out[...] = vector
    x_ref[0 : sh.cap, :] = vector.astype(BF16)
    if step == 0:
        code_ref = code_out[0]
        for c in range(sh.chunks):
            table = jnp.zeros((16, LANES), F32)
            for s in range(c * sh.per, (c + 1) * sh.per):
                table = table + recv_ref[s, sh.extra :, :].astype(F32)
            target = wrap(table[0:1].astype(jnp.int32), count)
            code = target * sh.noff + table[1:2].astype(jnp.int32)
            code_ref[c : c + 1, :] = jnp.where(table[2:3] > 0.5, code, -1)
    else:
        code_ref = code_in[0]
    for s in range(sh.tiles):
        parts = [recv_ref[s, p * sh.slots : (p + 1) * sh.slots, :] for p in range(sh.full)]
        end = recv_ref[s, sh.head : sh.extra, :].astype(F32)
        if sh.fold == 2:
            end = jnp.concatenate([end[:, : sh.rest], end[:, sh.rest :]], axis=0)
        else:
            end = end[:, : sh.rest]
        block = jnp.concatenate([part.astype(F32) for part in parts] + [end], axis=1)
        a = s * sh.slots
        row = next_vector(step, block, [ref[a : a + sh.slots, :] for ref in copies], sums)
        if copy_out is not None:
            copy_out[a : a + sh.slots, :] = row
        x_ref[sh.cap + a : sh.cap + a + sh.slots, :] = row.astype(BF16)
    field = jnp.zeros((sh.cap, sh.width), F32)
    mark = iota((sh.cap, LANES), 0) * sh.noff
    for g in range(groups):
        for q in range(GROUP):
            o = g * GROUP + q
            p_ref[q * sh.cap : (q + 1) * sh.cap, 0 : sh.cap] = pairs_ref[o]
            for c in range(sh.chunks):
                hit = (code_ref[c : c + 1, :] - o == mark).astype(F32).astype(BF16)
                p_ref[q * sh.cap : (q + 1) * sh.cap, sh.cap + c * LANES : sh.cap + (c + 1) * LANES] = hit
        summed = dot(p_ref[...], x_ref[...]).astype(BF16)
        loads[g].wait()
        for q in range(GROUP):
            field = field + dot(summed[q * sh.cap : (q + 1) * sh.cap], lattice_vmem[g * GROUP + q])
    live = (iota((sh.cap, 1), 0) < count).astype(F32)
    image = live * dot(field.astype(BF16), tmatrix_ref[...])
    image_out[...] = image
    out = [total(ref[...] * image) for ref in olds] + [total(vector * image), total(image * image)]
    row8 = iota((8, LANES), 0)
    seen = jnp.zeros((8, LANES), F32)
    for q, value in enumerate(sums):
        seen = jnp.where(row8 == q, value, seen)
    sums_out[...] = seen
    if last:
        tile = jnp.zeros((8, LANES), F32)
        for q, value in enumerate(out):
            tile = jnp.where(row8 == q, value, tile)
        for d in range(sh.tiles):
            send_out[d] = tile
    else:
        pack(sh, image.astype(BF16), rank_ref, send_out, sel_ref)
        tile = sum_rows(out).astype(BF16)
        for d in range(sh.tiles):
            send_out[d, sh.extra :, :] = tile


def last_kernel(sh, recv_ref, *refs):
    seen = refs[:ITERS]
    vectors = refs[ITERS : 2 * ITERS]
    image_ref, basis_ref, hess_ref = refs[2 * ITERS :]
    final = jnp.zeros((8, LANES), F32)
    for s in range(sh.tiles):
        final = final + recv_ref[s]
    tables = [ref[...] for ref in seen[1:]] + [final]
    row = iota((ITERS + 1, ITERS), 0)
    col = iota((ITERS + 1, ITERS), 1)
    hess = jnp.zeros((ITERS + 1, ITERS), F32)
    for k in range(ITERS):
        square = tables[k][k + 1 : k + 2, 0:1]
        for j in range(k + 1):
            product = tables[k][j : j + 1, 0:1]
            square = square - product * product
            hess = jnp.where((row == j) & (col == k), (1.0 if j == k else 0.0) - product, hess)
        hess = jnp.where((row == k + 1) & (col == k), jnp.sqrt(square), hess)
    hess_ref[...] = hess
    sums = [final[q : q + 1, 0:1] for q in range(ITERS + 1)]
    olds = [ref[...] for ref in vectors]
    for j in range(ITERS):
        basis_ref[j] = olds[j]
    basis_ref[ITERS] = next_vector(ITERS, image_ref[...], olds, sums)


def call(kernel, name, outs, args, smem=0, hbm=(), scratch=()):
    whole = pl.BlockSpec(memory_space=pltpu.VMEM)
    specs = [
        pl.BlockSpec(memory_space=pltpu.SMEM if i < smem else pl.ANY) if i < smem or i in hbm else whole
        for i in range(len(args))
    ]
    return pl.pallas_call(
        kernel,
        name=name,
        out_shape=[jax.ShapeDtypeStruct(shape, dtype) for shape, dtype in outs],
        in_specs=specs,
        out_specs=[whole] * len(outs),
        scratch_shapes=list(scratch),
        compiler_params=pltpu.CompilerParams(vmem_limit_bytes=VMEM_LIMIT),
    )(*args)


def per_device(
    rhs,
    counts,
    local_target,
    local_offset,
    remote_tile,
    remote_target,
    remote_offset,
    lattice,
    tmatrix,
):
    tiles = lax.axis_size("tile")
    cap, width = rhs.shape
    noff = lattice.shape[0]
    sh = Shape(tiles, cap, width, local_target.shape[1], remote_tile.shape[1], noff)
    mine = lax.axis_index("tile").astype(jnp.int32).reshape(1)
    exchange = functools.partial(
        lax.all_to_all, axis_name="tile", split_axis=0, concat_axis=0, tiled=True
    )
    own = ((cap, width), F32)
    block = ((tiles, sh.rows, LANES), BF16)
    select = pltpu.VMEM((sh.inbound, cap), BF16)
    start, rank, send = call(
        functools.partial(first_kernel, sh),
        "first",
        [own, ((tiles, cap), jnp.int32), block],
        [mine, counts, rhs, remote_tile, remote_target, remote_offset],
        smem=2,
        scratch=[select, pltpu.VMEM((tiles, cap), jnp.int32)],
    )
    recv = exchange(send)
    (pairs,) = call(
        functools.partial(local_kernel, sh),
        "local_pairs",
        [((noff, cap, cap), BF16)],
        [mine, counts, local_target, local_offset],
        smem=2,
        scratch=[pltpu.VMEM((sh.nl, cap), jnp.int32)],
    )
    current, olds, copies, codes, seen = start, [], [], [], []
    for step in range(ITERS):
        last = step == ITERS - 1
        outs = [own, own, ((8, LANES), F32)]
        outs.append(((tiles, 8, LANES), F32) if last else block)
        if not last:
            outs.append(((sh.inbound, width), F32))
        if step == 0:
            outs.append(((sh.chunks, LANES), jnp.int32))
        result = call(
            functools.partial(step_kernel, sh, step),
            f"step{step}",
            outs,
            [mine, counts, recv, rank, pairs, tmatrix, lattice, current, *olds, *copies, *codes],
            smem=2,
            hbm=(6,),
            scratch=[
                pltpu.VMEM((noff, width, width), BF16),
                pltpu.SemaphoreType.DMA((noff // GROUP,)),
                pltpu.VMEM((cap + sh.inbound, width), BF16),
                pltpu.VMEM((GROUP * cap, cap + sh.inbound), BF16),
                select,
            ],
        )
        vector, current, sums, send = result[:4]
        olds.append(vector)
        seen.append(sums)
        if not last:
            copies.append(result[4])
        if step == 0:
            codes = [result[5]]
        recv = exchange(send)
    basis, hess = call(
        functools.partial(last_kernel, sh),
        "last",
        [((ITERS + 1, cap, width), F32), ((ITERS + 1, ITERS), F32)],
        [recv, *seen, *olds, current],
    )
    return basis, hess


def solution(mesh):
    placed = (
        P(("groups", "tile"), None),
        P("groups"),
        P(("groups", "tile"), None),
        P(("groups", "tile"), None),
        P(("groups", "tile"), None),
        P(("groups", "tile"), None),
        P(("groups", "tile"), None),
        P(),
        P(),
    )
    return jax.shard_map(
        per_device,
        mesh=mesh,
        in_specs=placed,
        out_specs=(P(None, ("groups", "tile"), None), P("groups", None)),
        check_vma=False,
    )
```

```python
import functools

import jax
import jax.numpy as jnp
from jax import lax
from jax.experimental import pallas as pl
from jax.experimental.pallas import tpu as pltpu
from jax.sharding import PartitionSpec as P

ITERS = 3
LANES = 128
GROUP = 4
F32 = jnp.float32
BF16 = jnp.bfloat16
VMEM_LIMIT = 56 * 1024 * 1024


def iota(shape, dim):
    return lax.broadcasted_iota(jnp.int32, shape, dim)


def dot(a, b):
    return lax.dot_general(a, b, (((1,), (0,)), ((), ())), preferred_element_type=F32)


def dot_nt(a, b):
    return lax.dot_general(a, b, (((1,), (1,)), ((), ())), preferred_element_type=F32)


def dot_tn(a, b):
    return lax.dot_general(a, b, (((0,), (0,)), ((), ())), preferred_element_type=F32)


def flag(mask):
    return mask.astype(F32).astype(BF16)


def identity(size):
    return flag(iota((size, size), 0) == iota((size, size), 1))


def total(values):
    return jnp.sum(jnp.sum(values, axis=0, keepdims=True), axis=1, keepdims=True)


def pieces(value):
    first = value.astype(BF16).astype(F32)
    rest = value - first
    second = rest.astype(BF16).astype(F32)
    return first, second, rest - second


def wrap(target, count):
    for _ in range(3):
        target = jnp.where(target >= count, target - count, target)
    return target


def each(amount, body):
    if amount <= 16:
        for i in range(amount):
            body(i)
    else:
        lax.fori_loop(0, amount, lambda i, carry: (body(i), carry)[1], 0)


class Shape:
    def __init__(self, tiles, cap, width, nl, nr, noff):
        self.tiles, self.cap, self.width, self.nl, self.nr, self.noff = tiles, cap, width, nl, nr, noff
        self.send_cap = max(2, 2 * cap * nr // tiles)
        self.slots = max(16, self.send_cap)
        self.fold = LANES // self.slots
        self.part = width // self.fold
        self.extra = -(-self.part // 16) * 16
        self.rows = self.extra + 16
        self.chunks = tiles // self.fold
        self.inbound = self.chunks * LANES
        self.sources = cap + self.inbound


def pack(sh, mine, values, rank_ref, out_ref):
    parts = [values[f * sh.part : (f + 1) * sh.part] for f in range(sh.fold)]
    wide = jnp.concatenate(parts, axis=1)
    lane = iota((LANES, sh.cap), 0)
    shifts = [lax.rem(mine + f, sh.fold) * sh.slots for f in range(sh.fold)]

    def body(d):
        rank = rank_ref[pl.ds(d, 1), :]
        picked = jnp.concatenate([flag(rank + shift == lane) for shift in shifts], axis=1)
        block = dot_nt(wide, picked).astype(BF16)
        if sh.extra > sh.part:
            block = jnp.concatenate([block, jnp.zeros((sh.extra - sh.part, LANES), BF16)], axis=0)
        out_ref[d, 0 : sh.extra, :] = block

    each(sh.tiles, body)


def sum_rows(sums):
    row = iota((16, LANES), 0)
    tile = jnp.zeros((16, LANES), F32)
    for q, value in enumerate(sums):
        for p, piece in enumerate(pieces(value)):
            tile = jnp.where(row == 4 + 3 * q + p, piece, tile)
    return tile


def first_kernel(sh, mine_ref, counts_ref, rhs_ref, tile_ref, target_ref, offset_ref,
                 start_ref, rank_ref, out_ref, code_ref):
    mine = mine_ref[0]
    count = counts_ref[mine]
    start = rhs_ref[...] * (iota((1, sh.cap), 1) < count).astype(F32)
    start_ref[...] = start
    tile = tile_ref[...]
    target = target_ref[...].astype(F32)
    offset = offset_ref[...].astype(F32)
    which = iota((sh.tiles, sh.cap), 0)
    named = jnp.zeros((sh.tiles, sh.cap), F32)
    targets = jnp.zeros((sh.tiles, sh.cap), F32)
    offsets = jnp.zeros((sh.tiles, sh.cap), F32)
    for r in range(sh.nr):
        hit = tile[r : r + 1, :] == which
        named = jnp.where(hit, 1.0, named)
        targets = jnp.where(hit, target[r : r + 1, :], targets)
        offsets = jnp.where(hit, offset[r : r + 1, :], offsets)
    before = flag(iota((sh.cap, sh.cap), 0) < iota((sh.cap, sh.cap), 1))
    rank = dot(named.astype(BF16), before).astype(jnp.int32)
    rank_ref[...] = jnp.where(named > 0.0, rank, -2 * LANES)
    code_ref[0] = targets
    code_ref[1] = offsets
    code_ref[2] = named
    pack(sh, mine, start.astype(BF16), rank_ref, out_ref)
    sums = sum_rows([total(start * start)])
    shift = lax.rem(mine, sh.fold) * sh.slots
    row = iota((16, LANES), 0)
    lane = iota((LANES, sh.cap), 0)

    def body(d):
        picked = flag(rank_ref[pl.ds(d, 1), :] + shift == lane)
        table = jnp.zeros((16, sh.cap), F32)
        for q in range(3):
            table = jnp.where(row == q, code_ref[q, pl.ds(d, 1), :], table)
        extra = dot_nt(table.astype(BF16), picked) + sums
        out_ref[d, sh.extra :, :] = extra.astype(BF16)

    each(sh.tiles, body)


def tables_kernel(sh, mine_ref, counts_ref, target_ref, offset_ref, tmatrix_ref, lattice_ref,
                  pairs_ref, flipped_ref, turned_ref, code_ref, lattice_vmem, sems):
    groups = sh.noff // GROUP
    loads = [
        pltpu.make_async_copy(
            lattice_ref.at[pl.ds(g * GROUP, GROUP)], lattice_vmem.at[pl.ds(g * GROUP, GROUP)], sems.at[g]
        )
        for g in range(groups)
    ]
    for load in loads:
        load.start()
    count = counts_ref[mine_ref[0]]
    code_ref[...] = wrap(target_ref[...], count) * sh.noff + offset_ref[...]
    eye = identity(sh.cap)

    def body(o, carry):
        mark = iota((sh.cap, sh.cap), 0) * sh.noff + o
        amount = jnp.zeros((sh.cap, sh.cap), F32)
        for n in range(sh.nl):
            amount = amount + (code_ref[n : n + 1, :] == mark).astype(F32)
        pairs_ref[o] = dot_nt(eye, amount.astype(BF16)).astype(BF16)
        return carry

    lax.fori_loop(0, sh.noff, body, 0)
    wide = identity(sh.width)
    turned_ref[...] = dot_nt(wide, tmatrix_ref[...]).astype(BF16)
    for g in range(groups):
        loads[g].wait()
        some = lattice_vmem[g * GROUP : (g + 1) * GROUP].reshape(GROUP * sh.width, sh.width)
        span = GROUP * sh.width
        flipped_ref[:, g * span : (g + 1) * span] = dot_nt(wide, some).astype(BF16)


def next_vector(step, current, olds, sums):
    if step == 0:
        return current / jnp.sqrt(sums[0])
    square = sums[step]
    kept = current
    for j in range(step):
        square = square - sums[j] * sums[j]
        kept = kept - sums[j] * olds[j]
    return -kept / jnp.sqrt(square)


def step_kernel(sh, step, *refs):
    refs = list(refs)
    take = lambda n: [refs.pop(0) for _ in range(n)]
    mine_ref, counts_ref, recv_ref, rank_ref, pairs_ref, turned_ref, flipped_ref, current_ref = take(8)
    olds = take(step)
    copies = take(step)
    key_in = take(1 if step else 0)
    vector_out, image_out, sums_out, send_out = take(4)
    last = step == ITERS - 1
    copy_out = None if last else take(1)[0]
    key_out = take(0 if step else 1)
    flipped_vmem, sems, x_ref, p_ref = refs
    groups = sh.noff // GROUP
    span = GROUP * sh.width
    loads = [
        pltpu.make_async_copy(
            flipped_ref.at[:, pl.ds(g * span, span)], flipped_vmem.at[:, pl.ds(g * span, span)], sems.at[g]
        )
        for g in range(groups)
    ]
    for load in loads:
        load.start()
    mine = mine_ref[0]
    count = counts_ref[mine]
    extras = jnp.zeros((16, LANES), F32)
    for s in range(sh.tiles):
        extras = extras + recv_ref[s, sh.extra :, :].astype(F32)
    sums = []
    for q in range(max(1, step + 1)):
        r = 4 + 3 * q
        sums.append(extras[r : r + 1, 0:1] + extras[r + 1 : r + 2, 0:1] + extras[r + 2 : r + 3, 0:1])
    vector = next_vector(step, current_ref[...], [ref[...] for ref in olds], sums)
    vector_out[...] = vector
    x_ref[:, 0 : sh.cap] = vector.astype(BF16)
    if step == 0:
        key_ref = key_out[0]
        row = iota((16, LANES), 0)
        weight = jnp.where(row == 0, sh.noff, 0) + jnp.where(row == 1, 1, 0)
        weight = weight - jnp.where(row == 2, iota((16, LANES), 1) * sh.noff, 0)
        weight = (weight - jnp.where(row == 3, 16384, 0)).astype(F32).astype(BF16)
        for c in range(sh.chunks):
            table = jnp.zeros((16, LANES), F32)
            for s in range(c * sh.fold, (c + 1) * sh.fold):
                table = table + recv_ref[s, sh.extra :, :].astype(F32)
            target = wrap(table[0:1].astype(jnp.int32), count).astype(F32)
            empty = 1.0 - table[2:3]
            table = jnp.where(row == 0, target, table)
            table = jnp.where(row == 3, empty, jnp.where(row > 3, 0.0, table))
            key_ref[c * LANES : (c + 1) * LANES, :] = dot_tn(table.astype(BF16), weight)
    else:
        key_ref = key_in[0]
    lane_group = iota((1, LANES), 1) // sh.slots
    for c in range(sh.chunks):
        parts = []
        for f in range(sh.fold):
            part = recv_ref[c * sh.fold, 0 : sh.extra, :].astype(F32)[: sh.part]
            for m in range(1, sh.fold):
                other = recv_ref[c * sh.fold + m, 0 : sh.extra, :].astype(F32)[: sh.part]
                part = jnp.where(lane_group == (m + f) % sh.fold, other, part)
            if f:
                part = pltpu.roll(part, LANES - f * sh.slots, 1)
            parts.append(part)
        a = c * LANES
        column = next_vector(
            step, jnp.concatenate(parts, axis=0), [ref[:, a : a + LANES] for ref in copies], sums
        )
        if copy_out is not None:
            copy_out[:, a : a + LANES] = column
        x_ref[:, sh.cap + a : sh.cap + a + LANES] = column.astype(BF16)
    field = jnp.zeros((sh.width, sh.cap), F32)
    for g in range(groups):
        for q in range(GROUP):
            o = g * GROUP + q
            cols = slice(q * sh.cap, (q + 1) * sh.cap)
            p_ref[0 : sh.cap, cols] = pairs_ref[o]
            for c in range(sh.chunks):
                a = c * LANES
                p_ref[sh.cap + a : sh.cap + a + LANES, cols] = flag(key_ref[a : a + LANES, :] == float(o))
        summed = dot(x_ref[...], p_ref[...]).astype(BF16)
        stack = jnp.concatenate([summed[:, q * sh.cap : (q + 1) * sh.cap] for q in range(GROUP)], axis=0)
        loads[g].wait()
        field = field + dot(flipped_vmem[:, g * span : (g + 1) * span], stack)
    live = (iota((1, sh.cap), 1) < count).astype(F32)
    image = live * dot(turned_ref[...], field.astype(BF16))
    image_out[...] = image
    out = [total(ref[...] * image) for ref in olds] + [total(vector * image), total(image * image)]
    row8 = iota((8, LANES), 0)
    seen = jnp.zeros((8, LANES), F32)
    for q, value in enumerate(sums):
        seen = jnp.where(row8 == q, value, seen)
    sums_out[...] = seen
    if last:
        tile = jnp.zeros((8, LANES), F32)
        for q, value in enumerate(out):
            tile = jnp.where(row8 == q, value, tile)
        for d in range(sh.tiles):
            send_out[d] = tile
    else:
        pack(sh, mine, image.astype(BF16), rank_ref, send_out)
        tile = sum_rows(out).astype(BF16)
        for d in range(sh.tiles):
            send_out[d, sh.extra :, :] = tile


def last_kernel(sh, recv_ref, *refs):
    seen = refs[:ITERS]
    vectors = refs[ITERS : 2 * ITERS]
    image_ref, basis_ref, hess_ref = refs[2 * ITERS :]
    final = jnp.zeros((8, LANES), F32)
    for s in range(sh.tiles):
        final = final + recv_ref[s]
    tables = [ref[...] for ref in seen[1:]] + [final]
    row = iota((ITERS + 1, ITERS), 0)
    col = iota((ITERS + 1, ITERS), 1)
    hess = jnp.zeros((ITERS + 1, ITERS), F32)
    for k in range(ITERS):
        square = tables[k][k + 1 : k + 2, 0:1]
        for j in range(k + 1):
            product = tables[k][j : j + 1, 0:1]
            square = square - product * product
            hess = jnp.where((row == j) & (col == k), (1.0 if j == k else 0.0) - product, hess)
        hess = jnp.where((row == k + 1) & (col == k), jnp.sqrt(square), hess)
    hess_ref[...] = hess
    sums = [final[q : q + 1, 0:1] for q in range(ITERS + 1)]
    olds = [ref[...] for ref in vectors]
    for j in range(ITERS):
        basis_ref[j] = olds[j]
    basis_ref[ITERS] = next_vector(ITERS, image_ref[...], olds, sums)


def call(kernel, name, outs, args, smem=0, hbm=(), scratch=()):
    whole = pl.BlockSpec(memory_space=pltpu.VMEM)
    specs = [
        pl.BlockSpec(memory_space=pltpu.SMEM if i < smem else pl.ANY) if i < smem or i in hbm else whole
        for i in range(len(args))
    ]
    return pl.pallas_call(
        kernel,
        name=name,
        out_shape=[jax.ShapeDtypeStruct(shape, dtype) for shape, dtype in outs],
        in_specs=specs,
        out_specs=[whole] * len(outs),
        scratch_shapes=list(scratch),
        compiler_params=pltpu.CompilerParams(vmem_limit_bytes=VMEM_LIMIT),
    )(*args)


def per_device(
    rhs,
    counts,
    local_target,
    local_offset,
    remote_tile,
    remote_target,
    remote_offset,
    lattice,
    tmatrix,
):
    tiles = lax.axis_size("tile")
    cap, width = rhs.shape
    noff = lattice.shape[0]
    groups = noff // GROUP
    sh = Shape(tiles, cap, width, local_target.shape[1], remote_tile.shape[1], noff)
    mine = lax.axis_index("tile").astype(jnp.int32).reshape(1)
    exchange = functools.partial(
        lax.all_to_all, axis_name="tile", split_axis=0, concat_axis=0, tiled=True
    )
    own = ((width, cap), F32)
    block = ((tiles, sh.rows, LANES), BF16)
    start, rank, send = call(
        functools.partial(first_kernel, sh),
        "first",
        [own, ((tiles, cap), jnp.int32), block],
        [mine, counts, rhs.T, remote_tile.T, remote_target.T, remote_offset.T],
        smem=2,
        scratch=[pltpu.VMEM((3, tiles, cap), F32)],
    )
    recv = exchange(send)
    pairs, flipped, turned = call(
        functools.partial(tables_kernel, sh),
        "tables",
        [((noff, cap, cap), BF16), ((width, noff * width), BF16), ((width, width), BF16)],
        [mine, counts, local_target.T, local_offset.T, tmatrix, lattice],
        smem=2,
        hbm=(5,),
        scratch=[
            pltpu.VMEM((sh.nl, cap), jnp.int32),
            pltpu.VMEM((noff, width, width), BF16),
            pltpu.SemaphoreType.DMA((groups,)),
        ],
    )
    current, olds, copies, keys, seen = start, [], [], [], []
    for step in range(ITERS):
        last = step == ITERS - 1
        outs = [own, own, ((8, LANES), F32)]
        outs.append(((tiles, 8, LANES), F32) if last else block)
        if not last:
            outs.append(((width, sh.inbound), F32))
        if step == 0:
            outs.append(((sh.inbound, LANES), F32))
        result = call(
            functools.partial(step_kernel, sh, step),
            f"step{step}",
            outs,
            [mine, counts, recv, rank, pairs, turned, flipped, current, *olds, *copies, *keys],
            smem=2,
            hbm=(6,),
            scratch=[
                pltpu.VMEM((width, noff * width), BF16),
                pltpu.SemaphoreType.DMA((groups,)),
                pltpu.VMEM((width, sh.sources), BF16),
                pltpu.VMEM((sh.sources, GROUP * cap), BF16),
            ],
        )
        vector, current, sums, send = result[:4]
        olds.append(vector)
        seen.append(sums)
        if not last:
            copies.append(result[4])
        if step == 0:
            keys = [result[5]]
        recv = exchange(send)
    basis, hess = call(
        functools.partial(last_kernel, sh),
        "last",
        [((ITERS + 1, width, cap), F32), ((ITERS + 1, ITERS), F32)],
        [recv, *seen, *olds, current],
    )
    return jnp.transpose(basis, (0, 2, 1)), hess


def solution(mesh):
    placed = (
        P(("groups", "tile"), None),
        P("groups"),
        P(("groups", "tile"), None),
        P(("groups", "tile"), None),
        P(("groups", "tile"), None),
        P(("groups", "tile"), None),
        P(("groups", "tile"), None),
        P(),
        P(),
    )
    return jax.shard_map(
        per_device,
        mesh=mesh,
        in_specs=placed,
        out_specs=(P(None, ("groups", "tile"), None), P("groups", None)),
        check_vma=False,
    )
```

```python
import functools

import jax
import jax.numpy as jnp
from jax import lax
from jax.experimental import pallas as pl
from jax.experimental.pallas import tpu as pltpu
from jax.sharding import PartitionSpec as P

ITERS = 3
LANES = 128
GROUP = 4
F32 = jnp.float32
BF16 = jnp.bfloat16
VMEM_LIMIT = 28 * 1024 * 1024


def iota(shape, dim):
    return lax.broadcasted_iota(jnp.int32, shape, dim)


def dot(a, b):
    return lax.dot_general(a, b, (((1,), (0,)), ((), ())), preferred_element_type=F32)


def dot_nt(a, b):
    return lax.dot_general(a, b, (((1,), (1,)), ((), ())), preferred_element_type=F32)


def dot_tn(a, b):
    return lax.dot_general(a, b, (((0,), (0,)), ((), ())), preferred_element_type=F32)


def flag(mask):
    return mask.astype(F32).astype(BF16)


def identity(size):
    return flag(iota((size, size), 0) == iota((size, size), 1))


def total(values):
    return jnp.sum(jnp.sum(values, axis=0, keepdims=True), axis=1, keepdims=True)


def pieces(value):
    first = value.astype(BF16).astype(F32)
    rest = value - first
    second = rest.astype(BF16).astype(F32)
    return first, second, rest - second


def wrap(target, count):
    for _ in range(3):
        target = jnp.where(target >= count, target - count, target)
    return target


def each(amount, body):
    if amount <= 16:
        for i in range(amount):
            body(i)
    else:
        lax.fori_loop(0, amount, lambda i, carry: (body(i), carry)[1], 0)


class Shape:
    def __init__(self, tiles, cap, width, nl, nr, noff):
        self.tiles, self.cap, self.width, self.nl, self.nr, self.noff = tiles, cap, width, nl, nr, noff
        self.send_cap = max(2, 2 * cap * nr // tiles)
        self.slots = max(16, self.send_cap)
        self.fold = LANES // self.slots
        self.part = width // self.fold
        self.extra = -(-self.part // 16) * 16
        self.rows = self.extra + 16
        self.chunks = tiles // self.fold
        self.inbound = self.chunks * LANES
        self.sources = cap + self.inbound


def pack(sh, mine, values, rank_ref, out_ref):
    parts = [values[f * sh.part : (f + 1) * sh.part] for f in range(sh.fold)]
    wide = jnp.concatenate(parts, axis=1)
    lane = iota((LANES, sh.cap), 0)
    shifts = [lax.rem(mine + f, sh.fold) * sh.slots for f in range(sh.fold)]

    def body(d):
        rank = rank_ref[pl.ds(d, 1), :]
        picked = jnp.concatenate([flag(rank + shift == lane) for shift in shifts], axis=1)
        block = dot_nt(wide, picked).astype(BF16)
        if sh.extra > sh.part:
            block = jnp.concatenate([block, jnp.zeros((sh.extra - sh.part, LANES), BF16)], axis=0)
        out_ref[d, 0 : sh.extra, :] = block

    each(sh.tiles, body)


def sum_rows(sums):
    row = iota((16, LANES), 0)
    tile = jnp.zeros((16, LANES), F32)
    for q, value in enumerate(sums):
        for p, piece in enumerate(pieces(value)):
            tile = jnp.where(row == 4 + 3 * q + p, piece, tile)
    return tile


def first_kernel(sh, mine_ref, counts_ref, rhs_ref, tile_ref, target_ref, offset_ref,
                 start_ref, rank_ref, out_ref, code_ref):
    mine = mine_ref[0]
    count = counts_ref[mine]
    start = rhs_ref[...] * (iota((1, sh.cap), 1) < count).astype(F32)
    start_ref[...] = start
    tile = tile_ref[...]
    target = target_ref[...].astype(F32)
    offset = offset_ref[...].astype(F32)
    which = iota((sh.tiles, sh.cap), 0)
    named = jnp.zeros((sh.tiles, sh.cap), F32)
    targets = jnp.zeros((sh.tiles, sh.cap), F32)
    offsets = jnp.zeros((sh.tiles, sh.cap), F32)
    for r in range(sh.nr):
        hit = tile[r : r + 1, :] == which
        named = jnp.where(hit, 1.0, named)
        targets = jnp.where(hit, target[r : r + 1, :], targets)
        offsets = jnp.where(hit, offset[r : r + 1, :], offsets)
    before = flag(iota((sh.cap, sh.cap), 0) < iota((sh.cap, sh.cap), 1))
    rank = dot(named.astype(BF16), before).astype(jnp.int32)
    rank_ref[...] = jnp.where(named > 0.0, rank, -2 * LANES)
    code_ref[0] = targets
    code_ref[1] = offsets
    code_ref[2] = named
    pack(sh, mine, start.astype(BF16), rank_ref, out_ref)
    sums = sum_rows([total(start * start)])
    shift = lax.rem(mine, sh.fold) * sh.slots
    row = iota((16, LANES), 0)
    lane = iota((LANES, sh.cap), 0)

    def body(d):
        picked = flag(rank_ref[pl.ds(d, 1), :] + shift == lane)
        table = jnp.zeros((16, sh.cap), F32)
        for q in range(3):
            table = jnp.where(row == q, code_ref[q, pl.ds(d, 1), :], table)
        extra = dot_nt(table.astype(BF16), picked) + sums
        out_ref[d, sh.extra :, :] = extra.astype(BF16)

    each(sh.tiles, body)


def tables_kernel(sh, mine_ref, counts_ref, target_ref, offset_ref, tmatrix_ref, lattice_ref,
                  pairs_ref, flipped_ref, turned_ref, code_ref):
    groups = sh.noff // GROUP
    count = counts_ref[mine_ref[0]]
    code_ref[...] = wrap(target_ref[...], count) * sh.noff + offset_ref[...]
    eye = identity(sh.cap)

    def body(o, carry):
        mark = iota((sh.cap, sh.cap), 0) * sh.noff + o
        amount = jnp.zeros((sh.cap, sh.cap), F32)
        for n in range(sh.nl):
            amount = amount + (code_ref[n : n + 1, :] == mark).astype(F32)
        pairs_ref[o] = dot_nt(eye, amount.astype(BF16)).astype(BF16)
        return carry

    lax.fori_loop(0, sh.noff, body, 0)
    wide = identity(sh.width)
    turned_ref[...] = dot_nt(wide, tmatrix_ref[...]).astype(BF16)
    for g in range(groups):
        some = lattice_ref[g * GROUP : (g + 1) * GROUP].reshape(GROUP * sh.width, sh.width)
        span = GROUP * sh.width
        flipped_ref[:, g * span : (g + 1) * span] = dot_nt(wide, some).astype(BF16)


def next_vector(step, current, olds, sums):
    if step == 0:
        return current / jnp.sqrt(sums[0])
    square = sums[step]
    kept = current
    for j in range(step):
        square = square - sums[j] * sums[j]
        kept = kept - sums[j] * olds[j]
    return -kept / jnp.sqrt(square)


def step_kernel(sh, step, *refs):
    refs = list(refs)
    take = lambda n: [refs.pop(0) for _ in range(n)]
    mine_ref, counts_ref, recv_ref, rank_ref, pairs_ref, turned_ref, flipped_ref, current_ref = take(8)
    olds = take(step)
    copies = take(step)
    key_in = take(1 if step else 0)
    vector_out, image_out, sums_out, send_out = take(4)
    last = step == ITERS - 1
    copy_out = None if last else take(1)[0]
    key_out = take(0 if step else 1)
    x_ref, p_ref = refs
    groups = sh.noff // GROUP
    span = GROUP * sh.width
    mine = mine_ref[0]
    count = counts_ref[mine]
    extras = jnp.zeros((16, LANES), F32)
    for s in range(sh.tiles):
        extras = extras + recv_ref[s, sh.extra :, :].astype(F32)
    sums = []
    for q in range(max(1, step + 1)):
        r = 4 + 3 * q
        sums.append(extras[r : r + 1, 0:1] + extras[r + 1 : r + 2, 0:1] + extras[r + 2 : r + 3, 0:1])
    vector = next_vector(step, current_ref[...], [ref[...] for ref in olds], sums)
    vector_out[...] = vector
    x_ref[:, 0 : sh.cap] = vector.astype(BF16)
    if step == 0:
        key_ref = key_out[0]
        row = iota((16, LANES), 0)
        weight = jnp.where(row == 0, sh.noff, 0) + jnp.where(row == 1, 1, 0)
        weight = weight - jnp.where(row == 2, iota((16, LANES), 1) * sh.noff, 0)
        weight = (weight - jnp.where(row == 3, 16384, 0)).astype(F32).astype(BF16)
        for c in range(sh.chunks):
            table = jnp.zeros((16, LANES), F32)
            for s in range(c * sh.fold, (c + 1) * sh.fold):
                table = table + recv_ref[s, sh.extra :, :].astype(F32)
            target = wrap(table[0:1].astype(jnp.int32), count).astype(F32)
            empty = 1.0 - table[2:3]
            table = jnp.where(row == 0, target, table)
            table = jnp.where(row == 3, empty, jnp.where(row > 3, 0.0, table))
            key_ref[c * LANES : (c + 1) * LANES, :] = dot_tn(table.astype(BF16), weight)
    else:
        key_ref = key_in[0]
    lane_group = iota((1, LANES), 1) // sh.slots
    for c in range(sh.chunks):
        parts = []
        for f in range(sh.fold):
            part = recv_ref[c * sh.fold, 0 : sh.extra, :].astype(F32)[: sh.part]
            for m in range(1, sh.fold):
                other = recv_ref[c * sh.fold + m, 0 : sh.extra, :].astype(F32)[: sh.part]
                part = jnp.where(lane_group == (m + f) % sh.fold, other, part)
            if f:
                part = pltpu.roll(part, LANES - f * sh.slots, 1)
            parts.append(part)
        a = c * LANES
        column = next_vector(
            step, jnp.concatenate(parts, axis=0), [ref[:, a : a + LANES] for ref in copies], sums
        )
        if copy_out is not None:
            copy_out[:, a : a + LANES] = column
        x_ref[:, sh.cap + a : sh.cap + a + LANES] = column.astype(BF16)
    field = jnp.zeros((sh.width, sh.cap), F32)
    for g in range(groups):
        for q in range(GROUP):
            o = g * GROUP + q
            cols = slice(q * sh.cap, (q + 1) * sh.cap)
            p_ref[0 : sh.cap, cols] = pairs_ref[o]
            for c in range(sh.chunks):
                a = c * LANES
                p_ref[sh.cap + a : sh.cap + a + LANES, cols] = flag(key_ref[a : a + LANES, :] == float(o))
        summed = dot(x_ref[...], p_ref[...]).astype(BF16)
        stack = jnp.concatenate([summed[:, q * sh.cap : (q + 1) * sh.cap] for q in range(GROUP)], axis=0)
        field = field + dot(flipped_ref[:, g * span : (g + 1) * span], stack)
    live = (iota((1, sh.cap), 1) < count).astype(F32)
    image = live * dot(turned_ref[...], field.astype(BF16))
    image_out[...] = image
    out = [total(ref[...] * image) for ref in olds] + [total(vector * image), total(image * image)]
    row8 = iota((8, LANES), 0)
    seen = jnp.zeros((8, LANES), F32)
    for q, value in enumerate(sums):
        seen = jnp.where(row8 == q, value, seen)
    sums_out[...] = seen
    if last:
        tile = jnp.zeros((8, LANES), F32)
        for q, value in enumerate(out):
            tile = jnp.where(row8 == q, value, tile)
        for d in range(sh.tiles):
            send_out[d] = tile
    else:
        pack(sh, mine, image.astype(BF16), rank_ref, send_out)
        tile = sum_rows(out).astype(BF16)
        for d in range(sh.tiles):
            send_out[d, sh.extra :, :] = tile


def last_kernel(sh, recv_ref, *refs):
    seen = refs[:ITERS]
    vectors = refs[ITERS : 2 * ITERS]
    image_ref, basis_ref, hess_ref = refs[2 * ITERS :]
    final = jnp.zeros((8, LANES), F32)
    for s in range(sh.tiles):
        final = final + recv_ref[s]
    tables = [ref[...] for ref in seen[1:]] + [final]
    row = iota((ITERS + 1, ITERS), 0)
    col = iota((ITERS + 1, ITERS), 1)
    hess = jnp.zeros((ITERS + 1, ITERS), F32)
    for k in range(ITERS):
        square = tables[k][k + 1 : k + 2, 0:1]
        for j in range(k + 1):
            product = tables[k][j : j + 1, 0:1]
            square = square - product * product
            hess = jnp.where((row == j) & (col == k), (1.0 if j == k else 0.0) - product, hess)
        hess = jnp.where((row == k + 1) & (col == k), jnp.sqrt(square), hess)
    hess_ref[...] = hess
    sums = [final[q : q + 1, 0:1] for q in range(ITERS + 1)]
    olds = [ref[...] for ref in vectors]
    for j in range(ITERS):
        basis_ref[j] = olds[j]
    basis_ref[ITERS] = next_vector(ITERS, image_ref[...], olds, sums)


def call(kernel, name, outs, args, smem=0, out_hbm=(), scratch=()):
    whole = pl.BlockSpec(memory_space=pltpu.VMEM)
    specs, placed = [], []
    for i, arg in enumerate(args):
        space = pltpu.SMEM if i < smem else pltpu.VMEM
        specs.append(pl.BlockSpec(memory_space=space))
        placed.append(pltpu.with_memory_space_constraint(arg, space) if space is pltpu.VMEM else arg)
    return pl.pallas_call(
        kernel,
        name=name,
        out_shape=[
            jax.ShapeDtypeStruct(shape, dtype) if i in out_hbm else pltpu.VMEM(shape, dtype)
            for i, (shape, dtype) in enumerate(outs)
        ],
        in_specs=specs,
        out_specs=[whole] * len(outs),
        scratch_shapes=list(scratch),
        compiler_params=pltpu.CompilerParams(vmem_limit_bytes=VMEM_LIMIT),
    )(*placed)


def per_device(
    rhs,
    counts,
    local_target,
    local_offset,
    remote_tile,
    remote_target,
    remote_offset,
    lattice,
    tmatrix,
):
    tiles = lax.axis_size("tile")
    cap, width = rhs.shape
    noff = lattice.shape[0]
    sh = Shape(tiles, cap, width, local_target.shape[1], remote_tile.shape[1], noff)
    mine = lax.axis_index("tile").astype(jnp.int32).reshape(1)
    exchange = functools.partial(
        lax.all_to_all, axis_name="tile", split_axis=0, concat_axis=0, tiled=True
    )
    own = ((width, cap), F32)
    block = ((tiles, sh.rows, LANES), BF16)
    start, rank, send = call(
        functools.partial(first_kernel, sh),
        "first",
        [own, ((tiles, cap), jnp.int32), block],
        [mine, counts, rhs.T, remote_tile.T, remote_target.T, remote_offset.T],
        smem=2,
        scratch=[pltpu.VMEM((3, tiles, cap), F32)],
    )
    recv = exchange(send)
    pairs, flipped, turned = call(
        functools.partial(tables_kernel, sh),
        "tables",
        [((noff, cap, cap), BF16), ((width, noff * width), BF16), ((width, width), BF16)],
        [mine, counts, local_target.T, local_offset.T, tmatrix, lattice],
        smem=2,
        scratch=[pltpu.VMEM((sh.nl, cap), jnp.int32)],
    )
    current, olds, copies, keys, seen = start, [], [], [], []
    for step in range(ITERS):
        last = step == ITERS - 1
        outs = [own, own, ((8, LANES), F32)]
        outs.append(((tiles, 8, LANES), F32) if last else block)
        if not last:
            outs.append(((width, sh.inbound), F32))
        if step == 0:
            outs.append(((sh.inbound, LANES), F32))
        result = call(
            functools.partial(step_kernel, sh, step),
            f"step{step}",
            outs,
            [mine, counts, recv, rank, pairs, turned, flipped, current, *olds, *copies, *keys],
            smem=2,
            scratch=[
                pltpu.VMEM((width, sh.sources), BF16),
                pltpu.VMEM((sh.sources, GROUP * cap), BF16),
            ],
        )
        vector, current, sums, send = result[:4]
        olds.append(vector)
        seen.append(sums)
        if not last:
            copies.append(result[4])
        if step == 0:
            keys = [result[5]]
        recv = exchange(send)
    basis, hess = call(
        functools.partial(last_kernel, sh),
        "last",
        [((ITERS + 1, width, cap), F32), ((ITERS + 1, ITERS), F32)],
        [recv, *seen, *olds, current],
        out_hbm=(0, 1),
    )
    return jnp.transpose(basis, (0, 2, 1)), hess


def solution(mesh):
    placed = (
        P(("groups", "tile"), None),
        P("groups"),
        P(("groups", "tile"), None),
        P(("groups", "tile"), None),
        P(("groups", "tile"), None),
        P(("groups", "tile"), None),
        P(("groups", "tile"), None),
        P(),
        P(),
    )
    return jax.shard_map(
        per_device,
        mesh=mesh,
        in_specs=placed,
        out_specs=(P(None, ("groups", "tile"), None), P("groups", None)),
        check_vma=False,
    )
```

```python
import functools

import jax
import jax.numpy as jnp
from jax import lax
from jax.experimental import pallas as pl
from jax.experimental.pallas import tpu as pltpu
from jax.sharding import PartitionSpec as P

ITERS = 3
LANES = 128
GROUP = 4
F32 = jnp.float32
BF16 = jnp.bfloat16
VMEM_LIMIT = 28 * 1024 * 1024


def iota(shape, dim):
    return lax.broadcasted_iota(jnp.int32, shape, dim)


def dot(a, b):
    return lax.dot_general(a, b, (((1,), (0,)), ((), ())), preferred_element_type=F32)


def dot_nt(a, b):
    return lax.dot_general(a, b, (((1,), (1,)), ((), ())), preferred_element_type=F32)


def dot_tn(a, b):
    return lax.dot_general(a, b, (((0,), (0,)), ((), ())), preferred_element_type=F32)


def flag(mask):
    return mask.astype(F32).astype(BF16)


def identity(size):
    return flag(iota((size, size), 0) == iota((size, size), 1))


def total(values):
    return jnp.sum(jnp.sum(values, axis=0, keepdims=True), axis=1, keepdims=True)


def pieces(value):
    first = value.astype(BF16).astype(F32)
    rest = value - first
    second = rest.astype(BF16).astype(F32)
    return first, second, rest - second


def wrap(target, count):
    for _ in range(3):
        target = jnp.where(target >= count, target - count, target)
    return target


def each(amount, body):
    if amount <= 16:
        for i in range(amount):
            body(i)
    else:
        lax.fori_loop(0, amount, lambda i, carry: (body(i), carry)[1], 0)


class Shape:
    def __init__(self, tiles, cap, width, nl, nr, noff):
        self.tiles, self.cap, self.width, self.nl, self.nr, self.noff = tiles, cap, width, nl, nr, noff
        self.send_cap = max(2, 2 * cap * nr // tiles)
        self.slots = max(16, self.send_cap)
        self.fold = LANES // self.slots
        self.part = width // self.fold
        self.extra = -(-self.part // 16) * 16
        self.rows = self.extra + 16
        self.chunks = tiles // self.fold
        self.inbound = self.chunks * LANES
        self.sources = cap + self.inbound


def pack(sh, mine, values, rank_ref, out_ref):
    parts = [values[f * sh.part : (f + 1) * sh.part] for f in range(sh.fold)]
    wide = jnp.concatenate(parts, axis=1)
    lane = iota((LANES, sh.cap), 0)
    shifts = [lax.rem(mine + f, sh.fold) * sh.slots for f in range(sh.fold)]

    def body(d):
        rank = rank_ref[pl.ds(d, 1), :]
        picked = jnp.concatenate([flag(rank + shift == lane) for shift in shifts], axis=1)
        block = dot_nt(wide, picked).astype(BF16)
        if sh.extra > sh.part:
            block = jnp.concatenate([block, jnp.zeros((sh.extra - sh.part, LANES), BF16)], axis=0)
        out_ref[d, 0 : sh.extra, :] = block

    each(sh.tiles, body)


def sum_rows(sums):
    row = iota((16, LANES), 0)
    tile = jnp.zeros((16, LANES), F32)
    for q, value in enumerate(sums):
        for p, piece in enumerate(pieces(value)):
            tile = jnp.where(row == 4 + 3 * q + p, piece, tile)
    return tile


def first_kernel(sh, mine_ref, counts_ref, rhs_ref, tile_ref, target_ref, offset_ref,
                 start_ref, rank_ref, out_ref, code_ref):
    mine = mine_ref[0]
    count = counts_ref[mine]
    start = rhs_ref[...] * (iota((1, sh.cap), 1) < count).astype(F32)
    start_ref[...] = start
    tile = tile_ref[...]
    target = target_ref[...].astype(F32)
    offset = offset_ref[...].astype(F32)
    which = iota((sh.tiles, sh.cap), 0)
    named = jnp.zeros((sh.tiles, sh.cap), F32)
    targets = jnp.zeros((sh.tiles, sh.cap), F32)
    offsets = jnp.zeros((sh.tiles, sh.cap), F32)
    for r in range(sh.nr):
        hit = tile[r : r + 1, :] == which
        named = jnp.where(hit, 1.0, named)
        targets = jnp.where(hit, target[r : r + 1, :], targets)
        offsets = jnp.where(hit, offset[r : r + 1, :], offsets)
    before = flag(iota((sh.cap, sh.cap), 0) < iota((sh.cap, sh.cap), 1))
    rank = dot(named.astype(BF16), before).astype(jnp.int32)
    rank_ref[...] = jnp.where(named > 0.0, rank, -2 * LANES)
    code_ref[0] = targets
    code_ref[1] = offsets
    code_ref[2] = named
    pack(sh, mine, start.astype(BF16), rank_ref, out_ref)
    sums = sum_rows([total(start * start)])
    shift = lax.rem(mine, sh.fold) * sh.slots
    row = iota((16, LANES), 0)
    lane = iota((LANES, sh.cap), 0)

    def body(d):
        picked = flag(rank_ref[pl.ds(d, 1), :] + shift == lane)
        table = jnp.zeros((16, sh.cap), F32)
        for q in range(3):
            table = jnp.where(row == q, code_ref[q, pl.ds(d, 1), :], table)
        extra = dot_nt(table.astype(BF16), picked) + sums
        out_ref[d, sh.extra :, :] = extra.astype(BF16)

    each(sh.tiles, body)


def tables_kernel(sh, mine_ref, counts_ref, target_ref, offset_ref, tmatrix_ref, lattice_ref,
                  pairs_ref, flipped_ref, turned_ref, code_ref, lattice_vmem, sems):
    groups = sh.noff // GROUP
    loads = [
        pltpu.make_async_copy(
            lattice_ref.at[pl.ds(g * GROUP, GROUP)], lattice_vmem.at[pl.ds(g * GROUP, GROUP)], sems.at[g]
        )
        for g in range(groups)
    ]
    for load in loads:
        load.start()
    count = counts_ref[mine_ref[0]]
    code_ref[...] = wrap(target_ref[...], count) * sh.noff + offset_ref[...]
    eye = identity(sh.cap)

    def body(o, carry):
        mark = iota((sh.cap, sh.cap), 0) * sh.noff + o
        amount = jnp.zeros((sh.cap, sh.cap), F32)
        for n in range(sh.nl):
            amount = amount + (code_ref[n : n + 1, :] == mark).astype(F32)
        pairs_ref[o] = dot_nt(eye, amount.astype(BF16)).astype(BF16)
        return carry

    lax.fori_loop(0, sh.noff, body, 0)
    wide = identity(sh.width)
    turned_ref[...] = dot_nt(wide, tmatrix_ref[...]).astype(BF16)
    for g in range(groups):
        loads[g].wait()
        some = lattice_vmem[g * GROUP : (g + 1) * GROUP].reshape(GROUP * sh.width, sh.width)
        span = GROUP * sh.width
        flipped_ref[:, g * span : (g + 1) * span] = dot_nt(wide, some).astype(BF16)


def next_vector(step, current, olds, sums):
    if step == 0:
        return current / jnp.sqrt(sums[0])
    square = sums[step]
    kept = current
    for j in range(step):
        square = square - sums[j] * sums[j]
        kept = kept - sums[j] * olds[j]
    return -kept / jnp.sqrt(square)


def step_kernel(sh, step, *refs):
    refs = list(refs)
    take = lambda n: [refs.pop(0) for _ in range(n)]
    mine_ref, counts_ref, recv_ref, rank_ref, pairs_ref, turned_ref, flipped_ref, current_ref = take(8)
    olds = take(step)
    copies = take(step)
    key_in = take(1 if step else 0)
    vector_out, image_out, sums_out, send_out = take(4)
    last = step == ITERS - 1
    copy_out = None if last else take(1)[0]
    key_out = take(0 if step else 1)
    x_ref = refs[0]
    groups = sh.noff // GROUP
    span = GROUP * sh.width
    mine = mine_ref[0]
    count = counts_ref[mine]
    extras = jnp.zeros((16, LANES), F32)
    for s in range(sh.tiles):
        extras = extras + recv_ref[s, sh.extra :, :].astype(F32)
    sums = []
    for q in range(max(1, step + 1)):
        r = 4 + 3 * q
        sums.append(extras[r : r + 1, 0:1] + extras[r + 1 : r + 2, 0:1] + extras[r + 2 : r + 3, 0:1])
    vector = next_vector(step, current_ref[...], [ref[...] for ref in olds], sums)
    vector_out[...] = vector
    x_ref[:, 0 : sh.cap] = vector.astype(BF16)
    if step == 0:
        key_ref = key_out[0]
        row = iota((16, LANES), 0)
        weight = jnp.where(row == 0, sh.noff, 0) + jnp.where(row == 1, 1, 0)
        weight = weight - jnp.where(row == 2, iota((16, LANES), 1) * sh.noff, 0)
        weight = (weight - jnp.where(row == 3, 16384, 0)).astype(F32).astype(BF16)
        for c in range(sh.chunks):
            table = jnp.zeros((16, LANES), F32)
            for s in range(c * sh.fold, (c + 1) * sh.fold):
                table = table + recv_ref[s, sh.extra :, :].astype(F32)
            target = wrap(table[0:1].astype(jnp.int32), count).astype(F32)
            empty = 1.0 - table[2:3]
            table = jnp.where(row == 0, target, table)
            table = jnp.where(row == 3, empty, jnp.where(row > 3, 0.0, table))
            key = dot_tn(table.astype(BF16), weight)
            key = jnp.where((key >= 0.0) & (key < sh.noff), key, -1.0)
            key_ref[c * LANES : (c + 1) * LANES, :] = key.astype(BF16)
    else:
        key_ref = key_in[0]
    lane_group = iota((1, LANES), 1) // sh.slots
    for c in range(sh.chunks):
        parts = []
        for f in range(sh.fold):
            part = recv_ref[c * sh.fold, 0 : sh.extra, :].astype(F32)[: sh.part]
            for m in range(1, sh.fold):
                other = recv_ref[c * sh.fold + m, 0 : sh.extra, :].astype(F32)[: sh.part]
                part = jnp.where(lane_group == (m + f) % sh.fold, other, part)
            if f:
                part = pltpu.roll(part, LANES - f * sh.slots, 1)
            parts.append(part)
        a = c * LANES
        column = next_vector(
            step, jnp.concatenate(parts, axis=0), [ref[:, a : a + LANES] for ref in copies], sums
        )
        if copy_out is not None:
            copy_out[:, a : a + LANES] = column
        x_ref[:, sh.cap + a : sh.cap + a + LANES] = column.astype(BF16)
    field = jnp.zeros((sh.width, sh.cap), F32)
    one, zero = jnp.ones((), BF16), jnp.zeros((), BF16)
    for g in range(groups):
        counts_of = []
        for o in range(g * GROUP, (g + 1) * GROUP):
            hits = jnp.where(key_ref[...] == jnp.asarray(o, BF16), one, zero)
            counts_of.append(jnp.concatenate([pairs_ref[o], hits], axis=0))
        summed = dot(x_ref[...], jnp.concatenate(counts_of, axis=1)).astype(BF16)
        stack = jnp.concatenate([summed[:, q * sh.cap : (q + 1) * sh.cap] for q in range(GROUP)], axis=0)
        field = field + dot(flipped_ref[:, g * span : (g + 1) * span], stack)
    live = (iota((1, sh.cap), 1) < count).astype(F32)
    image = live * dot(turned_ref[...], field.astype(BF16))
    image_out[...] = image
    out = [total(ref[...] * image) for ref in olds] + [total(vector * image), total(image * image)]
    row8 = iota((8, LANES), 0)
    seen = jnp.zeros((8, LANES), F32)
    for q, value in enumerate(sums):
        seen = jnp.where(row8 == q, value, seen)
    sums_out[...] = seen
    if last:
        tile = jnp.zeros((8, LANES), F32)
        for q, value in enumerate(out):
            tile = jnp.where(row8 == q, value, tile)
        for d in range(sh.tiles):
            send_out[d] = tile
    else:
        pack(sh, mine, image.astype(BF16), rank_ref, send_out)
        tile = sum_rows(out).astype(BF16)
        for d in range(sh.tiles):
            send_out[d, sh.extra :, :] = tile


def last_kernel(sh, recv_ref, *refs):
    seen = refs[:ITERS]
    vectors = refs[ITERS : 2 * ITERS]
    image_ref, basis_ref, hess_ref = refs[2 * ITERS :]
    final = jnp.zeros((8, LANES), F32)
    for s in range(sh.tiles):
        final = final + recv_ref[s]
    tables = [ref[...] for ref in seen[1:]] + [final]
    row = iota((ITERS + 1, ITERS), 0)
    col = iota((ITERS + 1, ITERS), 1)
    hess = jnp.zeros((ITERS + 1, ITERS), F32)
    for k in range(ITERS):
        square = tables[k][k + 1 : k + 2, 0:1]
        for j in range(k + 1):
            product = tables[k][j : j + 1, 0:1]
            square = square - product * product
            hess = jnp.where((row == j) & (col == k), (1.0 if j == k else 0.0) - product, hess)
        hess = jnp.where((row == k + 1) & (col == k), jnp.sqrt(square), hess)
    hess_ref[...] = hess
    sums = [final[q : q + 1, 0:1] for q in range(ITERS + 1)]
    olds = [ref[...] for ref in vectors]
    for j in range(ITERS):
        basis_ref[j] = olds[j]
    basis_ref[ITERS] = next_vector(ITERS, image_ref[...], olds, sums)


def call(kernel, name, outs, args, smem=0, plain=False, hbm=(), out_hbm=(), scratch=()):
    whole = pl.BlockSpec(memory_space=pltpu.VMEM)
    specs, placed = [], []
    for i, arg in enumerate(args):
        space = pltpu.SMEM if i < smem else pl.ANY if i in hbm else pltpu.VMEM
        specs.append(pl.BlockSpec(memory_space=space))
        held = pltpu.HBM if i < smem or plain else pltpu.VMEM
        placed.append(pltpu.with_memory_space_constraint(arg, held))
    return pl.pallas_call(
        kernel,
        name=name,
        out_shape=[
            jax.ShapeDtypeStruct(shape, dtype) if i in out_hbm else pltpu.VMEM(shape, dtype)
            for i, (shape, dtype) in enumerate(outs)
        ],
        in_specs=specs,
        out_specs=[whole] * len(outs),
        scratch_shapes=list(scratch),
        compiler_params=pltpu.CompilerParams(vmem_limit_bytes=VMEM_LIMIT),
    )(*placed)


def per_device(
    rhs,
    counts,
    local_target,
    local_offset,
    remote_tile,
    remote_target,
    remote_offset,
    lattice,
    tmatrix,
):
    tiles = lax.axis_size("tile")
    cap, width = rhs.shape
    noff = lattice.shape[0]
    sh = Shape(tiles, cap, width, local_target.shape[1], remote_tile.shape[1], noff)
    mine = lax.axis_index("tile").astype(jnp.int32).reshape(1)
    exchange = functools.partial(
        lax.all_to_all, axis_name="tile", split_axis=0, concat_axis=0, tiled=True
    )
    own = ((width, cap), F32)
    block = ((tiles, sh.rows, LANES), BF16)
    start, rank, send = call(
        functools.partial(first_kernel, sh),
        "first",
        [own, ((tiles, cap), jnp.int32), block],
        [mine, counts, rhs.T, remote_tile.T, remote_target.T, remote_offset.T],
        smem=2,
        plain=True,
        scratch=[pltpu.VMEM((3, tiles, cap), F32)],
    )
    recv = exchange(send)
    pairs, flipped, turned = call(
        functools.partial(tables_kernel, sh),
        "tables",
        [((noff, cap, cap), BF16), ((width, noff * width), BF16), ((width, width), BF16)],
        [mine, counts, local_target.T, local_offset.T, tmatrix, lattice],
        smem=2,
        plain=True,
        hbm=(5,),
        scratch=[
            pltpu.VMEM((sh.nl, cap), jnp.int32),
            pltpu.VMEM((noff, width, width), BF16),
            pltpu.SemaphoreType.DMA((noff // GROUP,)),
        ],
    )
    current, olds, copies, keys, seen = start, [], [], [], []
    for step in range(ITERS):
        last = step == ITERS - 1
        outs = [own, own, ((8, LANES), F32)]
        outs.append(((tiles, 8, LANES), F32) if last else block)
        if not last:
            outs.append(((width, sh.inbound), F32))
        if step == 0:
            outs.append(((sh.inbound, LANES), BF16))
        result = call(
            functools.partial(step_kernel, sh, step),
            f"step{step}",
            outs,
            [mine, counts, recv, rank, pairs, turned, flipped, current, *olds, *copies, *keys],
            smem=2,
            scratch=[pltpu.VMEM((width, sh.sources), BF16)],
        )
        vector, current, sums, send = result[:4]
        olds.append(vector)
        seen.append(sums)
        if not last:
            copies.append(result[4])
        if step == 0:
            keys = [result[5]]
        recv = exchange(send)
    basis, hess = call(
        functools.partial(last_kernel, sh),
        "last",
        [((ITERS + 1, width, cap), F32), ((ITERS + 1, ITERS), F32)],
        [recv, *seen, *olds, current],
        out_hbm=(0, 1),
    )
    return jnp.transpose(basis, (0, 2, 1)), hess


def solution(mesh):
    placed = (
        P(("groups", "tile"), None),
        P("groups"),
        P(("groups", "tile"), None),
        P(("groups", "tile"), None),
        P(("groups", "tile"), None),
        P(("groups", "tile"), None),
        P(("groups", "tile"), None),
        P(),
        P(),
    )
    return jax.shard_map(
        per_device,
        mesh=mesh,
        in_specs=placed,
        out_specs=(P(None, ("groups", "tile"), None), P("groups", None)),
        check_vma=False,
    )
```

```python
import functools

import jax
import jax.numpy as jnp
from jax import lax
from jax.experimental import pallas as pl
from jax.experimental.pallas import tpu as pltpu
from jax.sharding import PartitionSpec as P

ITERS = 3
LANES = 128
GROUP = 4
AHEAD = 2
F32 = jnp.float32
BF16 = jnp.bfloat16
VMEM_LIMIT = 28 * 1024 * 1024


def iota(shape, dim):
    return lax.broadcasted_iota(jnp.int32, shape, dim)


def dot(a, b):
    return lax.dot_general(a, b, (((1,), (0,)), ((), ())), preferred_element_type=F32)


def dot_nt(a, b):
    return lax.dot_general(a, b, (((1,), (1,)), ((), ())), preferred_element_type=F32)


def dot_tn(a, b):
    return lax.dot_general(a, b, (((0,), (0,)), ((), ())), preferred_element_type=F32)


def flag(mask):
    return mask.astype(F32).astype(BF16)


def identity(size):
    return flag(iota((size, size), 0) == iota((size, size), 1))


def total(values):
    return jnp.sum(jnp.sum(values, axis=0, keepdims=True), axis=1, keepdims=True)


def pieces(value):
    first = value.astype(BF16).astype(F32)
    rest = value - first
    second = rest.astype(BF16).astype(F32)
    return first, second, rest - second


def wrap(target, count):
    for _ in range(3):
        target = jnp.where(target >= count, target - count, target)
    return target


def each(amount, body):
    if amount <= 16:
        for i in range(amount):
            body(i)
    else:
        lax.fori_loop(0, amount, lambda i, carry: (body(i), carry)[1], 0)


class Shape:
    def __init__(self, tiles, cap, width, nl, nr, noff):
        self.tiles, self.cap, self.width, self.nl, self.nr, self.noff = tiles, cap, width, nl, nr, noff
        self.send_cap = max(2, 2 * cap * nr // tiles)
        self.slots = max(16, self.send_cap)
        self.fold = LANES // self.slots
        self.part = width // self.fold
        self.extra = -(-self.part // 16) * 16
        self.rows = self.extra + 16
        self.chunks = tiles // self.fold
        self.inbound = self.chunks * LANES
        self.sources = cap + self.inbound


def pack(sh, mine, values, rank_ref, out_ref):
    parts = [values[f * sh.part : (f + 1) * sh.part] for f in range(sh.fold)]
    wide = jnp.concatenate(parts, axis=1)
    lane = iota((LANES, sh.cap), 0)
    shifts = [lax.rem(mine + f, sh.fold) * sh.slots for f in range(sh.fold)]

    def body(d):
        rank = rank_ref[pl.ds(d, 1), :]
        picked = jnp.concatenate([flag(rank + shift == lane) for shift in shifts], axis=1)
        block = dot_nt(wide, picked).astype(BF16)
        if sh.extra > sh.part:
            block = jnp.concatenate([block, jnp.zeros((sh.extra - sh.part, LANES), BF16)], axis=0)
        out_ref[d, 0 : sh.extra, :] = block

    each(sh.tiles, body)


def sum_rows(sums):
    row = iota((16, LANES), 0)
    tile = jnp.zeros((16, LANES), F32)
    for q, value in enumerate(sums):
        for p, piece in enumerate(pieces(value)):
            tile = jnp.where(row == 4 + 3 * q + p, piece, tile)
    return tile


def first_kernel(sh, mine_ref, counts_ref, rhs_ref, tile_ref, target_ref, offset_ref,
                 start_ref, rank_ref, out_ref, code_ref):
    mine = mine_ref[0]
    count = counts_ref[mine]
    start = rhs_ref[...] * (iota((1, sh.cap), 1) < count).astype(F32)
    start_ref[...] = start
    tile = tile_ref[...]
    target = target_ref[...].astype(F32)
    offset = offset_ref[...].astype(F32)
    which = iota((sh.tiles, sh.cap), 0)
    named = jnp.zeros((sh.tiles, sh.cap), F32)
    targets = jnp.zeros((sh.tiles, sh.cap), F32)
    offsets = jnp.zeros((sh.tiles, sh.cap), F32)
    for r in range(sh.nr):
        hit = tile[r : r + 1, :] == which
        named = jnp.where(hit, 1.0, named)
        targets = jnp.where(hit, target[r : r + 1, :], targets)
        offsets = jnp.where(hit, offset[r : r + 1, :], offsets)
    before = flag(iota((sh.cap, sh.cap), 0) < iota((sh.cap, sh.cap), 1))
    rank = dot(named.astype(BF16), before).astype(jnp.int32)
    rank_ref[...] = jnp.where(named > 0.0, rank, -2 * LANES)
    code_ref[0] = targets
    code_ref[1] = offsets
    code_ref[2] = named
    pack(sh, mine, start.astype(BF16), rank_ref, out_ref)
    sums = sum_rows([total(start * start)])
    shift = lax.rem(mine, sh.fold) * sh.slots
    row = iota((16, LANES), 0)
    lane = iota((LANES, sh.cap), 0)

    def body(d):
        picked = flag(rank_ref[pl.ds(d, 1), :] + shift == lane)
        table = jnp.zeros((16, sh.cap), F32)
        for q in range(3):
            table = jnp.where(row == q, code_ref[q, pl.ds(d, 1), :], table)
        extra = dot_nt(table.astype(BF16), picked) + sums
        out_ref[d, sh.extra :, :] = extra.astype(BF16)

    each(sh.tiles, body)


def slot_keys(sh, target, offset, empty):
    rows = iota((16, target.shape[1]), 0)
    table = jnp.where(rows == 0, target, 0.0)
    table = jnp.where(rows == 1, offset, table)
    table = jnp.where(rows == 2, 1.0, table)
    if empty is not None:
        table = jnp.where(rows == 3, empty, table)
    row, col = iota((16, sh.cap), 0), iota((16, sh.cap), 1)
    weight = jnp.where(row == 0, sh.noff, 0) + jnp.where(row == 1, 1, 0)
    weight = weight - jnp.where(row == 2, col * sh.noff, 0) - jnp.where(row == 3, 16384, 0)
    key = dot_tn(table.astype(BF16), weight.astype(F32).astype(BF16))
    return jnp.where((key >= 0.0) & (key < sh.noff), key, -1.0).astype(BF16)


def matches(keys, o):
    return jnp.where(keys == o, jnp.ones((), BF16), jnp.zeros((), BF16))


def tables_kernel(sh, mine_ref, counts_ref, target_ref, offset_ref, tmatrix_ref, lattice_ref, *refs):
    pairs_ref, turned_ref, flipped_ref, key_ref, lattice_vmem, flipped_vmem, sems, out_sems = refs
    groups = sh.noff // GROUP
    loads = [
        pltpu.make_async_copy(
            lattice_ref.at[pl.ds(g * GROUP, GROUP)], lattice_vmem.at[pl.ds(g * GROUP, GROUP)], sems.at[g]
        )
        for g in range(groups)
    ]
    for load in loads:
        load.start()
    count = counts_ref[mine_ref[0]]
    target = wrap(target_ref[...], count).astype(F32)
    offset = offset_ref[...].astype(F32)
    for n in range(sh.nl):
        key_ref[n] = slot_keys(sh, target[n : n + 1, :], offset[n : n + 1, :], None)
    for o in range(sh.noff):
        amount = matches(key_ref[0], jnp.asarray(o, BF16))
        for n in range(1, sh.nl):
            amount = amount + matches(key_ref[n], jnp.asarray(o, BF16))
        pairs_ref[o] = amount
    wide = identity(sh.width)
    turned_ref[...] = dot_nt(wide, tmatrix_ref[...]).astype(BF16)
    span = GROUP * sh.width
    stores = []
    for g in range(groups):
        loads[g].wait()
        some = lattice_vmem[g * GROUP : (g + 1) * GROUP].reshape(span, sh.width)
        flipped_vmem[g] = dot_nt(wide, some).astype(BF16)
        stores.append(pltpu.make_async_copy(flipped_vmem.at[g], flipped_ref.at[g], out_sems.at[g]))
        stores[g].start()
    for store in stores:
        store.wait()


def next_vector(step, current, olds, sums):
    if step == 0:
        return current / jnp.sqrt(sums[0])
    square = sums[step]
    kept = current
    for j in range(step):
        square = square - sums[j] * sums[j]
        kept = kept - sums[j] * olds[j]
    return -kept / jnp.sqrt(square)


def step_kernel(sh, step, *refs):
    refs = list(refs)
    take = lambda n: [refs.pop(0) for _ in range(n)]
    mine_ref, counts_ref, recv_ref, rank_ref, pairs_ref, turned_ref = take(6)
    flipped_ref, current_ref = take(2)
    olds = take(step)
    copies = take(step)
    key_in = take(1 if step else 0)
    vector_out, image_out, sums_out, send_out = take(4)
    last = step == ITERS - 1
    copy_out = None if last else take(1)[0]
    key_out = take(0 if step else 1)
    flipped_out = take(0 if step else 1)
    x_ref, *sems = refs
    groups = sh.noff // GROUP
    loads = []
    if step == 0:
        source, flipped_ref = flipped_ref, flipped_out[0]
        loads = [pltpu.make_async_copy(source.at[g], flipped_ref.at[g], sems[0].at[g]) for g in range(groups)]
    for load in loads[:AHEAD]:
        load.start()
    mine = mine_ref[0]
    count = counts_ref[mine]
    extras = jnp.zeros((16, LANES), F32)
    for s in range(sh.tiles):
        extras = extras + recv_ref[s, sh.extra :, :].astype(F32)
    sums = []
    for q in range(max(1, step + 1)):
        r = 4 + 3 * q
        sums.append(extras[r : r + 1, 0:1] + extras[r + 1 : r + 2, 0:1] + extras[r + 2 : r + 3, 0:1])
    vector = next_vector(step, current_ref[...], [ref[...] for ref in olds], sums)
    vector_out[...] = vector
    x_ref[:, 0 : sh.cap] = vector.astype(BF16)
    if step == 0:
        key_ref = key_out[0]
        for c in range(sh.chunks):
            table = jnp.zeros((16, LANES), F32)
            for s in range(c * sh.fold, (c + 1) * sh.fold):
                table = table + recv_ref[s, sh.extra :, :].astype(F32)
            target = wrap(table[0:1].astype(jnp.int32), count).astype(F32)
            key_ref[c * LANES : (c + 1) * LANES, :] = slot_keys(sh, target, table[1:2], 1.0 - table[2:3])
    else:
        key_ref = key_in[0]
    lane_group = iota((1, LANES), 1) // sh.slots
    for c in range(sh.chunks):
        parts = []
        for f in range(sh.fold):
            part = recv_ref[c * sh.fold, 0 : sh.extra, :].astype(F32)[: sh.part]
            for m in range(1, sh.fold):
                other = recv_ref[c * sh.fold + m, 0 : sh.extra, :].astype(F32)[: sh.part]
                part = jnp.where(lane_group == (m + f) % sh.fold, other, part)
            if f:
                part = pltpu.roll(part, LANES - f * sh.slots, 1)
            parts.append(part)
        a = c * LANES
        column = next_vector(
            step, jnp.concatenate(parts, axis=0), [ref[:, a : a + LANES] for ref in copies], sums
        )
        if copy_out is not None:
            copy_out[:, a : a + LANES] = column
        x_ref[:, sh.cap + a : sh.cap + a + LANES] = column.astype(BF16)
    field = jnp.zeros((sh.width, sh.cap), F32)
    for g in range(groups):
        counts_of = []
        for o in range(g * GROUP, (g + 1) * GROUP):
            hits = matches(key_ref[...], jnp.asarray(o, BF16))
            counts_of.append(jnp.concatenate([pairs_ref[o], hits], axis=0))
        summed = dot(x_ref[...], jnp.concatenate(counts_of, axis=1)).astype(BF16)
        stack = jnp.concatenate([summed[:, q * sh.cap : (q + 1) * sh.cap] for q in range(GROUP)], axis=0)
        if loads:
            loads[g].wait()
            if g + AHEAD < groups:
                loads[g + AHEAD].start()
        field = field + dot(flipped_ref[g], stack)
    live = (iota((1, sh.cap), 1) < count).astype(F32)
    image = live * dot(turned_ref[...], field.astype(BF16))
    image_out[...] = image
    out = [total(ref[...] * image) for ref in olds] + [total(vector * image), total(image * image)]
    row8 = iota((8, LANES), 0)
    seen = jnp.zeros((8, LANES), F32)
    for q, value in enumerate(sums):
        seen = jnp.where(row8 == q, value, seen)
    sums_out[...] = seen
    if last:
        tile = jnp.zeros((8, LANES), F32)
        for q, value in enumerate(out):
            tile = jnp.where(row8 == q, value, tile)
        for d in range(sh.tiles):
            send_out[d] = tile
    else:
        pack(sh, mine, image.astype(BF16), rank_ref, send_out)
        tile = sum_rows(out).astype(BF16)
        for d in range(sh.tiles):
            send_out[d, sh.extra :, :] = tile


def last_kernel(sh, recv_ref, *refs):
    seen = refs[:ITERS]
    vectors = refs[ITERS : 2 * ITERS]
    image_ref, basis_ref, hess_ref = refs[2 * ITERS :]
    final = jnp.zeros((8, LANES), F32)
    for s in range(sh.tiles):
        final = final + recv_ref[s]
    tables = [ref[...] for ref in seen[1:]] + [final]
    row = iota((ITERS + 1, ITERS), 0)
    col = iota((ITERS + 1, ITERS), 1)
    hess = jnp.zeros((ITERS + 1, ITERS), F32)
    for k in range(ITERS):
        square = tables[k][k + 1 : k + 2, 0:1]
        for j in range(k + 1):
            product = tables[k][j : j + 1, 0:1]
            square = square - product * product
            hess = jnp.where((row == j) & (col == k), (1.0 if j == k else 0.0) - product, hess)
        hess = jnp.where((row == k + 1) & (col == k), jnp.sqrt(square), hess)
    hess_ref[...] = hess
    sums = [final[q : q + 1, 0:1] for q in range(ITERS + 1)]
    olds = [ref[...] for ref in vectors]
    for j in range(ITERS):
        basis_ref[j] = olds[j]
    basis_ref[ITERS] = next_vector(ITERS, image_ref[...], olds, sums)


def call(kernel, name, outs, args, smem=0, plain=False, hbm=(), out_hbm=(), out_plain=(), scratch=()):
    specs, placed = [], []
    for i, arg in enumerate(args):
        space = pltpu.SMEM if i < smem else pl.ANY if i in hbm else pltpu.VMEM
        specs.append(pl.BlockSpec(memory_space=space))
        held = pltpu.HBM if i < smem or plain or i in hbm else pltpu.VMEM
        placed.append(pltpu.with_memory_space_constraint(arg, held))
    return pl.pallas_call(
        kernel,
        name=name,
        out_shape=[
            pltpu.HBM(shape, dtype) if i in out_plain or i in out_hbm else pltpu.VMEM(shape, dtype)
            for i, (shape, dtype) in enumerate(outs)
        ],
        in_specs=specs,
        out_specs=[
            pl.BlockSpec(memory_space=pl.ANY if i in out_hbm else pltpu.VMEM) for i in range(len(outs))
        ],
        scratch_shapes=list(scratch),
        compiler_params=pltpu.CompilerParams(vmem_limit_bytes=VMEM_LIMIT),
    )(*placed)


def per_device(
    rhs,
    counts,
    local_target,
    local_offset,
    remote_tile,
    remote_target,
    remote_offset,
    lattice,
    tmatrix,
):
    tiles = lax.axis_size("tile")
    cap, width = rhs.shape
    noff = lattice.shape[0]
    sh = Shape(tiles, cap, width, local_target.shape[1], remote_tile.shape[1], noff)
    mine = lax.axis_index("tile").astype(jnp.int32).reshape(1)
    exchange = functools.partial(
        lax.all_to_all, axis_name="tile", split_axis=0, concat_axis=0, tiled=True
    )
    own = ((width, cap), F32)
    block = ((tiles, sh.rows, LANES), BF16)
    groups = noff // GROUP
    lattice_shape = (groups, width, GROUP * width)
    start, rank, send = call(
        functools.partial(first_kernel, sh),
        "first",
        [own, ((tiles, cap), jnp.int32), block],
        [mine, counts, rhs.T, remote_tile.T, remote_target.T, remote_offset.T],
        smem=2,
        plain=True,
        scratch=[pltpu.VMEM((3, tiles, cap), F32)],
    )
    recv = exchange(send)
    pairs, turned, flipped = call(
        functools.partial(tables_kernel, sh),
        "tables",
        [((noff, cap, cap), BF16), ((width, width), BF16), (lattice_shape, BF16)],
        [mine, counts, local_target.T, local_offset.T, tmatrix, lattice],
        smem=2,
        plain=True,
        hbm=(5,),
        out_hbm=(2,),
        scratch=[
            pltpu.VMEM((sh.nl, cap, cap), BF16),
            pltpu.VMEM((noff, width, width), BF16),
            pltpu.VMEM(lattice_shape, BF16),
            pltpu.SemaphoreType.DMA((groups,)),
            pltpu.SemaphoreType.DMA((groups,)),
        ],
    )
    current, olds, copies, keys, seen = start, [], [], [], []
    for step in range(ITERS):
        last = step == ITERS - 1
        outs = [own, own, ((8, LANES), F32)]
        outs.append(((tiles, 8, LANES), F32) if last else block)
        if not last:
            outs.append(((width, sh.inbound), F32))
        if step == 0:
            outs.append(((sh.inbound, LANES), BF16))
            outs.append((lattice_shape, BF16))
        result = call(
            functools.partial(step_kernel, sh, step),
            f"step{step}",
            outs,
            [mine, counts, recv, rank, pairs, turned, flipped, current, *olds, *copies, *keys],
            smem=2,
            hbm=() if step else (6,),
            scratch=[pltpu.VMEM((width, sh.sources), BF16)]
            + ([] if step else [pltpu.SemaphoreType.DMA((groups,))]),
        )
        vector, current, sums, send = result[:4]
        olds.append(vector)
        seen.append(sums)
        if not last:
            copies.append(result[4])
        if step == 0:
            keys, flipped = [result[5]], result[6]
        recv = exchange(send)
    basis, hess = call(
        functools.partial(last_kernel, sh),
        "last",
        [((ITERS + 1, width, cap), F32), ((ITERS + 1, ITERS), F32)],
        [recv, *seen, *olds, current],
        out_plain=(0, 1),
    )
    return jnp.transpose(basis, (0, 2, 1)), hess


def solution(mesh):
    placed = (
        P(("groups", "tile"), None),
        P("groups"),
        P(("groups", "tile"), None),
        P(("groups", "tile"), None),
        P(("groups", "tile"), None),
        P(("groups", "tile"), None),
        P(("groups", "tile"), None),
        P(),
        P(),
    )
    return jax.shard_map(
        per_device,
        mesh=mesh,
        in_specs=placed,
        out_specs=(P(None, ("groups", "tile"), None), P("groups", None)),
        check_vma=False,
    )
```

```python
import functools

import jax
import jax.numpy as jnp
from jax import lax
from jax.experimental import pallas as pl
from jax.experimental.pallas import tpu as pltpu
from jax.sharding import PartitionSpec as P

ITERS = 3
LANES = 128
GROUP = 8
AHEAD = 2
F32 = jnp.float32
BF16 = jnp.bfloat16
VMEM_LIMIT = 28 * 1024 * 1024


def iota(shape, dim):
    return lax.broadcasted_iota(jnp.int32, shape, dim)


def dot(a, b):
    return lax.dot_general(a, b, (((1,), (0,)), ((), ())), preferred_element_type=F32)


def dot_nt(a, b):
    return lax.dot_general(a, b, (((1,), (1,)), ((), ())), preferred_element_type=F32)


def dot_tn(a, b):
    return lax.dot_general(a, b, (((0,), (0,)), ((), ())), preferred_element_type=F32)


def flag(mask):
    return mask.astype(F32).astype(BF16)


def identity(size):
    return flag(iota((size, size), 0) == iota((size, size), 1))


def total(values):
    return jnp.sum(jnp.sum(values, axis=0, keepdims=True), axis=1, keepdims=True)


def pieces(value):
    first = value.astype(BF16).astype(F32)
    rest = value - first
    second = rest.astype(BF16).astype(F32)
    return first, second, rest - second


def wrap(target, count):
    for _ in range(3):
        target = jnp.where(target >= count, target - count, target)
    return target


def each(amount, body):
    if amount <= 16:
        for i in range(amount):
            body(i)
    else:
        lax.fori_loop(0, amount, lambda i, carry: (body(i), carry)[1], 0)


class Shape:
    def __init__(self, tiles, cap, width, nl, nr, noff):
        self.tiles, self.cap, self.width, self.nl, self.nr, self.noff = tiles, cap, width, nl, nr, noff
        self.send_cap = max(2, 2 * cap * nr // tiles)
        self.slots = max(16, self.send_cap)
        self.fold = LANES // self.slots
        self.part = width // self.fold
        self.extra = -(-self.part // 8) * 8
        self.rows = self.extra + 8
        self.chunks = tiles // self.fold
        self.inbound = self.chunks * LANES
        self.sources = cap + self.inbound


def pack(sh, mine, values, rank_ref, out_ref, extra):
    parts = [values[f * sh.part : (f + 1) * sh.part] for f in range(sh.fold)]
    wide = jnp.concatenate(parts, axis=1)
    lane = iota((LANES, sh.cap), 0)
    shifts = [lax.rem(mine + f, sh.fold) * sh.slots for f in range(sh.fold)]

    def body(d):
        rank = rank_ref[pl.ds(d, 1), :]
        picked = [flag(rank + shift == lane) for shift in shifts]
        block = [dot_nt(wide, jnp.concatenate(picked, axis=1))]
        if sh.extra > sh.part:
            block.append(jnp.zeros((sh.extra - sh.part, LANES), F32))
        block.append(extra(d, picked[0]))
        out_ref[d] = jnp.concatenate(block, axis=0).astype(BF16)

    each(sh.tiles, body)


def sum_rows(sums):
    row, col = iota((8, LANES), 0), iota((8, LANES), 1)
    tile = jnp.zeros((8, LANES), F32)
    for q, value in enumerate(sums):
        first, second, third = pieces(value)
        spread = jnp.where(col < 32, first, jnp.where(col < 64, second, third))
        tile = jnp.where(row == 4 + q, spread, tile)
    return tile


def first_kernel(sh, mine_ref, counts_ref, rhs_ref, tile_ref, target_ref, offset_ref,
                 start_ref, rank_ref, out_ref, code_ref):
    mine = mine_ref[0]
    count = counts_ref[mine]
    start = rhs_ref[...] * (iota((1, sh.cap), 1) < count).astype(F32)
    start_ref[...] = start
    tile = tile_ref[...]
    target = target_ref[...].astype(F32)
    offset = offset_ref[...].astype(F32)
    which = iota((sh.tiles, sh.cap), 0)
    named = jnp.zeros((sh.tiles, sh.cap), F32)
    targets = jnp.zeros((sh.tiles, sh.cap), F32)
    offsets = jnp.zeros((sh.tiles, sh.cap), F32)
    for r in range(sh.nr):
        hit = tile[r : r + 1, :] == which
        named = jnp.where(hit, 1.0, named)
        targets = jnp.where(hit, target[r : r + 1, :], targets)
        offsets = jnp.where(hit, offset[r : r + 1, :], offsets)
    before = flag(iota((sh.cap, sh.cap), 0) < iota((sh.cap, sh.cap), 1))
    rank = dot(named.astype(BF16), before).astype(jnp.int32)
    rank_ref[...] = jnp.where(named > 0.0, rank, -2 * LANES)
    code_ref[0] = targets
    code_ref[1] = offsets
    code_ref[2] = named
    sums = sum_rows([total(start * start)])
    row = iota((8, LANES), 0)

    def extra(d, picked):
        table = jnp.zeros((8, sh.cap), F32)
        for q in range(3):
            table = jnp.where(row == q, code_ref[q, pl.ds(d, 1), :], table)
        return dot_nt(table.astype(BF16), picked) + sums

    pack(sh, mine, start.astype(BF16), rank_ref, out_ref, extra)


def slot_keys(sh, target, offset, empty):
    rows = iota((16, target.shape[1]), 0)
    table = jnp.where(rows == 0, target, 0.0)
    table = jnp.where(rows == 1, offset, table)
    table = jnp.where(rows == 2, 1.0, table)
    if empty is not None:
        table = jnp.where(rows == 3, empty, table)
    row, col = iota((16, sh.cap), 0), iota((16, sh.cap), 1)
    weight = jnp.where(row == 0, sh.noff, 0) + jnp.where(row == 1, 1, 0)
    weight = weight - jnp.where(row == 2, col * sh.noff, 0) - jnp.where(row == 3, 16384, 0)
    key = dot_tn(table.astype(BF16), weight.astype(F32).astype(BF16))
    return jnp.where((key >= 0.0) & (key < sh.noff), key, -1.0).astype(BF16)


def matches(keys, o):
    return jnp.where(keys == o, jnp.ones((), BF16), jnp.zeros((), BF16))


def tables_kernel(sh, mine_ref, counts_ref, target_ref, offset_ref, tmatrix_ref, lattice_ref, *refs):
    pairs_ref, turned_ref, flipped_ref, key_ref, lattice_vmem, flipped_vmem, sems, out_sems = refs
    groups = sh.noff // GROUP
    loads = [
        pltpu.make_async_copy(
            lattice_ref.at[pl.ds(g * GROUP, GROUP)], lattice_vmem.at[pl.ds(g * GROUP, GROUP)], sems.at[g]
        )
        for g in range(groups)
    ]
    for load in loads:
        load.start()
    count = counts_ref[mine_ref[0]]
    target = wrap(target_ref[...], count).astype(F32)
    offset = offset_ref[...].astype(F32)
    for n in range(sh.nl):
        key_ref[n] = slot_keys(sh, target[n : n + 1, :], offset[n : n + 1, :], None)
    for o in range(sh.noff):
        amount = matches(key_ref[0], jnp.asarray(o, BF16))
        for n in range(1, sh.nl):
            amount = amount + matches(key_ref[n], jnp.asarray(o, BF16))
        pairs_ref[o] = amount
    wide = identity(sh.width)
    turned_ref[...] = dot_nt(wide, tmatrix_ref[...]).astype(BF16)
    span = GROUP * sh.width
    stores = []
    for g in range(groups):
        loads[g].wait()
        some = lattice_vmem[g * GROUP : (g + 1) * GROUP].reshape(span, sh.width)
        flipped_vmem[g] = dot_nt(wide, some).astype(BF16)
        stores.append(pltpu.make_async_copy(flipped_vmem.at[g], flipped_ref.at[g], out_sems.at[g]))
        stores[g].start()
    for store in stores:
        store.wait()


def next_vector(step, current, olds, sums):
    if step == 0:
        return current / jnp.sqrt(sums[0])
    square = sums[step]
    kept = current
    for j in range(step):
        square = square - sums[j] * sums[j]
        kept = kept - sums[j] * olds[j]
    return -kept / jnp.sqrt(square)


def step_kernel(sh, step, *refs):
    refs = list(refs)
    take = lambda n: [refs.pop(0) for _ in range(n)]
    mine_ref, counts_ref, recv_ref, rank_ref, pairs_ref, turned_ref = take(6)
    flipped_ref, current_ref = take(2)
    olds = take(step)
    copies = take(step)
    key_in = take(1 if step else 0)
    vector_out, image_out, sums_out, send_out = take(4)
    last = step == ITERS - 1
    copy_out = None if last else take(1)[0]
    key_out = take(0 if step else 1)
    flipped_out = take(0 if step else 1)
    x_ref, *sems = refs
    groups = sh.noff // GROUP
    loads = []
    if step == 0:
        source, flipped_ref = flipped_ref, flipped_out[0]
        loads = [pltpu.make_async_copy(source.at[g], flipped_ref.at[g], sems[0].at[g]) for g in range(groups)]
    for load in loads[:AHEAD]:
        load.start()
    mine = mine_ref[0]
    count = counts_ref[mine]
    extras = jnp.zeros((8, LANES), F32)
    for s in range(sh.tiles):
        extras = extras + recv_ref[s].astype(F32)[sh.extra :]
    sums = []
    for q in range(max(1, step + 1)):
        r = extras[4 + q : 5 + q]
        sums.append(r[:, 0:1] + r[:, 32:33] + r[:, 64:65])
    vector = next_vector(step, current_ref[...], [ref[...] for ref in olds], sums)
    vector_out[...] = vector
    x_ref[:, 0 : sh.cap] = vector.astype(BF16)
    if step == 0:
        key_ref = key_out[0]
        for c in range(sh.chunks):
            table = jnp.zeros((8, LANES), F32)
            for s in range(c * sh.fold, (c + 1) * sh.fold):
                table = table + recv_ref[s].astype(F32)[sh.extra :]
            target = wrap(table[0:1].astype(jnp.int32), count).astype(F32)
            key_ref[c * LANES : (c + 1) * LANES, :] = slot_keys(sh, target, table[1:2], 1.0 - table[2:3])
    else:
        key_ref = key_in[0]
    lane_group = iota((1, LANES), 1) // sh.slots
    for c in range(sh.chunks):
        parts = []
        for f in range(sh.fold):
            part = recv_ref[c * sh.fold].astype(F32)[: sh.part]
            for m in range(1, sh.fold):
                other = recv_ref[c * sh.fold + m].astype(F32)[: sh.part]
                part = jnp.where(lane_group == (m + f) % sh.fold, other, part)
            if f:
                part = pltpu.roll(part, LANES - f * sh.slots, 1)
            parts.append(part)
        a = c * LANES
        column = next_vector(
            step, jnp.concatenate(parts, axis=0), [ref[:, a : a + LANES] for ref in copies], sums
        )
        if copy_out is not None:
            copy_out[:, a : a + LANES] = column
        x_ref[:, sh.cap + a : sh.cap + a + LANES] = column.astype(BF16)
    field = jnp.zeros((sh.width, sh.cap), F32)
    for g in range(groups):
        counts_of = []
        for o in range(g * GROUP, (g + 1) * GROUP):
            hits = matches(key_ref[...], jnp.asarray(o, BF16))
            counts_of.append(jnp.concatenate([pairs_ref[o], hits], axis=0))
        summed = dot(x_ref[...], jnp.concatenate(counts_of, axis=1)).astype(BF16)
        stack = jnp.concatenate([summed[:, q * sh.cap : (q + 1) * sh.cap] for q in range(GROUP)], axis=0)
        if loads:
            loads[g].wait()
            if g + AHEAD < groups:
                loads[g + AHEAD].start()
        field = field + dot(flipped_ref[g], stack)
    live = (iota((1, sh.cap), 1) < count).astype(F32)
    image = live * dot(turned_ref[...], field.astype(BF16))
    image_out[...] = image
    out = [total(ref[...] * image) for ref in olds] + [total(vector * image), total(image * image)]
    row8 = iota((8, LANES), 0)
    seen = jnp.zeros((8, LANES), F32)
    for q, value in enumerate(sums):
        seen = jnp.where(row8 == q, value, seen)
    sums_out[...] = seen
    if last:
        tile = jnp.zeros((8, LANES), F32)
        for q, value in enumerate(out):
            tile = jnp.where(row8 == q, value, tile)
        for d in range(sh.tiles):
            send_out[d] = tile
    else:
        tile = sum_rows(out)
        pack(sh, mine, image.astype(BF16), rank_ref, send_out, lambda d, picked: tile)


def last_kernel(sh, recv_ref, *refs):
    seen = refs[:ITERS]
    vectors = refs[ITERS : 2 * ITERS]
    image_ref, basis_ref, hess_ref = refs[2 * ITERS :]
    final = jnp.zeros((8, LANES), F32)
    for s in range(sh.tiles):
        final = final + recv_ref[s]
    tables = [ref[...] for ref in seen[1:]] + [final]
    row = iota((ITERS + 1, ITERS), 0)
    col = iota((ITERS + 1, ITERS), 1)
    hess = jnp.zeros((ITERS + 1, ITERS), F32)
    for k in range(ITERS):
        square = tables[k][k + 1 : k + 2, 0:1]
        for j in range(k + 1):
            product = tables[k][j : j + 1, 0:1]
            square = square - product * product
            hess = jnp.where((row == j) & (col == k), (1.0 if j == k else 0.0) - product, hess)
        hess = jnp.where((row == k + 1) & (col == k), jnp.sqrt(square), hess)
    hess_ref[...] = hess
    sums = [final[q : q + 1, 0:1] for q in range(ITERS + 1)]
    olds = [ref[...] for ref in vectors]
    for j in range(ITERS):
        basis_ref[j] = olds[j]
    basis_ref[ITERS] = next_vector(ITERS, image_ref[...], olds, sums)


def call(kernel, name, outs, args, smem=0, plain=False, hbm=(), out_hbm=(), out_plain=(), scratch=()):
    specs, placed = [], []
    for i, arg in enumerate(args):
        space = pltpu.SMEM if i < smem else pl.ANY if i in hbm else pltpu.VMEM
        specs.append(pl.BlockSpec(memory_space=space))
        held = pltpu.HBM if i < smem or plain or i in hbm else pltpu.VMEM
        placed.append(pltpu.with_memory_space_constraint(arg, held))
    return pl.pallas_call(
        kernel,
        name=name,
        out_shape=[
            pltpu.HBM(shape, dtype) if i in out_plain or i in out_hbm else pltpu.VMEM(shape, dtype)
            for i, (shape, dtype) in enumerate(outs)
        ],
        in_specs=specs,
        out_specs=[
            pl.BlockSpec(memory_space=pl.ANY if i in out_hbm else pltpu.VMEM) for i in range(len(outs))
        ],
        scratch_shapes=list(scratch),
        compiler_params=pltpu.CompilerParams(vmem_limit_bytes=VMEM_LIMIT),
    )(*placed)


def per_device(
    rhs,
    counts,
    local_target,
    local_offset,
    remote_tile,
    remote_target,
    remote_offset,
    lattice,
    tmatrix,
):
    tiles = lax.axis_size("tile")
    cap, width = rhs.shape
    noff = lattice.shape[0]
    sh = Shape(tiles, cap, width, local_target.shape[1], remote_tile.shape[1], noff)
    mine = lax.axis_index("tile").astype(jnp.int32).reshape(1)
    exchange = functools.partial(
        lax.all_to_all, axis_name="tile", split_axis=0, concat_axis=0, tiled=True
    )
    own = ((width, cap), F32)
    block = ((tiles, sh.rows, LANES), BF16)
    groups = noff // GROUP
    lattice_shape = (groups, width, GROUP * width)
    start, rank, send = call(
        functools.partial(first_kernel, sh),
        "first",
        [own, ((tiles, cap), jnp.int32), block],
        [mine, counts, rhs.T, remote_tile.T, remote_target.T, remote_offset.T],
        smem=2,
        plain=True,
        scratch=[pltpu.VMEM((3, tiles, cap), F32)],
    )
    recv = exchange(send)
    pairs, turned, flipped = call(
        functools.partial(tables_kernel, sh),
        "tables",
        [((noff, cap, cap), BF16), ((width, width), BF16), (lattice_shape, BF16)],
        [mine, counts, local_target.T, local_offset.T, tmatrix, lattice],
        smem=2,
        plain=True,
        hbm=(5,),
        out_hbm=(2,),
        scratch=[
            pltpu.VMEM((sh.nl, cap, cap), BF16),
            pltpu.VMEM((noff, width, width), BF16),
            pltpu.VMEM(lattice_shape, BF16),
            pltpu.SemaphoreType.DMA((groups,)),
            pltpu.SemaphoreType.DMA((groups,)),
        ],
    )
    current, olds, copies, keys, seen = start, [], [], [], []
    for step in range(ITERS):
        last = step == ITERS - 1
        outs = [own, own, ((8, LANES), F32)]
        outs.append(((tiles, 8, LANES), F32) if last else block)
        if not last:
            outs.append(((width, sh.inbound), F32))
        if step == 0:
            outs.append(((sh.inbound, LANES), BF16))
            outs.append((lattice_shape, BF16))
        result = call(
            functools.partial(step_kernel, sh, step),
            f"step{step}",
            outs,
            [mine, counts, recv, rank, pairs, turned, flipped, current, *olds, *copies, *keys],
            smem=2,
            hbm=() if step else (6,),
            scratch=[pltpu.VMEM((width, sh.sources), BF16)]
            + ([] if step else [pltpu.SemaphoreType.DMA((groups,))]),
        )
        vector, current, sums, send = result[:4]
        olds.append(vector)
        seen.append(sums)
        if not last:
            copies.append(result[4])
        if step == 0:
            keys, flipped = [result[5]], result[6]
        recv = exchange(send)
    basis, hess = call(
        functools.partial(last_kernel, sh),
        "last",
        [((ITERS + 1, width, cap), F32), ((ITERS + 1, ITERS), F32)],
        [recv, *seen, *olds, current],
        out_plain=(0, 1),
    )
    return jnp.transpose(basis, (0, 2, 1)), hess


def solution(mesh):
    placed = (
        P(("groups", "tile"), None),
        P("groups"),
        P(("groups", "tile"), None),
        P(("groups", "tile"), None),
        P(("groups", "tile"), None),
        P(("groups", "tile"), None),
        P(("groups", "tile"), None),
        P(),
        P(),
    )
    return jax.shard_map(
        per_device,
        mesh=mesh,
        in_specs=placed,
        out_specs=(P(None, ("groups", "tile"), None), P("groups", None)),
        check_vma=False,
    )
```

```python
import functools

import jax
import jax.numpy as jnp
from jax import lax
from jax.experimental import pallas as pl
from jax.experimental.pallas import tpu as pltpu
from jax.sharding import PartitionSpec as P

ITERS = 3
LANES = 128
GROUP = 8
AHEAD = 2
F32 = jnp.float32
BF16 = jnp.bfloat16
VMEM_LIMIT = 28 * 1024 * 1024


def iota(shape, dim):
    return lax.broadcasted_iota(jnp.int32, shape, dim)


def dot(a, b):
    return lax.dot_general(a, b, (((1,), (0,)), ((), ())), preferred_element_type=F32)


def dot_nt(a, b):
    return lax.dot_general(a, b, (((1,), (1,)), ((), ())), preferred_element_type=F32)


def dot_tn(a, b):
    return lax.dot_general(a, b, (((0,), (0,)), ((), ())), preferred_element_type=F32)


def flag(mask):
    return mask.astype(F32).astype(BF16)


def identity(size):
    return flag(iota((size, size), 0) == iota((size, size), 1))


def total(values):
    return jnp.sum(jnp.sum(values, axis=0, keepdims=True), axis=1, keepdims=True)


def pieces(value):
    first = value.astype(BF16).astype(F32)
    rest = value - first
    second = rest.astype(BF16).astype(F32)
    return first, second, rest - second


def wrap(target, count):
    for _ in range(3):
        target = jnp.where(target >= count, target - count, target)
    return target


def each(amount, body):
    if amount <= 16:
        for i in range(amount):
            body(i)
    else:
        lax.fori_loop(0, amount, lambda i, carry: (body(i), carry)[1], 0)


class Shape:
    def __init__(self, tiles, cap, width, nl, nr, noff):
        self.tiles, self.cap, self.width, self.nl, self.nr, self.noff = tiles, cap, width, nl, nr, noff
        self.send_cap = max(2, 2 * cap * nr // tiles)
        self.slots = max(16, self.send_cap)
        self.fold = LANES // self.slots
        self.part = width // self.fold
        self.extra = -(-self.part // 8) * 8
        self.rows = self.extra + 8
        self.chunks = tiles // self.fold
        self.inbound = self.chunks * LANES
        self.window = -(-self.inbound * 3 // 8 // LANES) * LANES
        self.groups = noff // GROUP
        self.sources = cap + self.inbound


def pack(sh, mine, values, rank_ref, out_ref, extra):
    parts = [values[f * sh.part : (f + 1) * sh.part] for f in range(sh.fold)]
    wide = jnp.concatenate(parts, axis=1)
    lane = iota((LANES, sh.cap), 0)
    shifts = [lax.rem(mine + f, sh.fold) * sh.slots for f in range(sh.fold)]

    def body(d):
        rank = rank_ref[pl.ds(d, 1), :]
        picked = [flag(rank + shift == lane) for shift in shifts]
        block = [dot_nt(wide, jnp.concatenate(picked, axis=1))]
        if sh.extra > sh.part:
            block.append(jnp.zeros((sh.extra - sh.part, LANES), F32))
        block.append(extra(d, picked[0]))
        out_ref[d] = jnp.concatenate(block, axis=0).astype(BF16)

    each(sh.tiles, body)


def sum_rows(sums):
    row, col = iota((8, LANES), 0), iota((8, LANES), 1)
    tile = jnp.zeros((8, LANES), F32)
    for q, value in enumerate(sums):
        first, second, third = pieces(value)
        spread = jnp.where(col < 32, first, jnp.where(col < 64, second, third))
        tile = jnp.where(row == 4 + q, spread, tile)
    return tile


def first_kernel(sh, mine_ref, counts_ref, rhs_ref, tile_ref, target_ref, offset_ref,
                 start_ref, rank_ref, out_ref, code_ref):
    mine = mine_ref[0]
    count = counts_ref[mine]
    live = (iota((1, sh.cap), 1) < count).astype(F32)
    start = rhs_ref[...] * live
    start_ref[...] = start
    tile = tile_ref[...]
    target = target_ref[...].astype(F32)
    offset = offset_ref[...].astype(F32)
    which = iota((sh.tiles, sh.cap), 0)
    named = jnp.zeros((sh.tiles, sh.cap), F32)
    targets = jnp.zeros((sh.tiles, sh.cap), F32)
    offsets = jnp.zeros((sh.tiles, sh.cap), F32)
    for r in range(sh.nr):
        hit = tile[r : r + 1, :] == which
        named = jnp.where(hit, live, named)
        targets = jnp.where(hit, target[r : r + 1, :], targets)
        offsets = jnp.where(hit, offset[r : r + 1, :], offsets)
    before = flag(iota((sh.cap, sh.cap), 0) < iota((sh.cap, sh.cap), 1))
    rank = dot(named.astype(BF16), before).astype(jnp.int32)
    rank_ref[...] = jnp.where(named > 0.0, rank, -2 * LANES)
    code_ref[0] = targets
    code_ref[1] = offsets
    code_ref[2] = named
    sums = sum_rows([total(start * start)])
    row = iota((8, LANES), 0)

    def extra(d, picked):
        table = jnp.zeros((8, sh.cap), F32)
        for q in range(3):
            table = jnp.where(row == q, code_ref[q, pl.ds(d, 1), :], table)
        return dot_nt(table.astype(BF16), picked) + sums

    pack(sh, mine, start.astype(BF16), rank_ref, out_ref, extra)


def slot_keys(sh, target, offset, empty):
    rows = iota((16, target.shape[1]), 0)
    table = jnp.where(rows == 0, target, 0.0)
    table = jnp.where(rows == 1, offset, table)
    table = jnp.where(rows == 2, 1.0, table)
    if empty is not None:
        table = jnp.where(rows == 3, empty, table)
    row, col = iota((16, sh.cap), 0), iota((16, sh.cap), 1)
    weight = jnp.where(row == 0, sh.noff, 0) + jnp.where(row == 1, 1, 0)
    weight = weight - jnp.where(row == 2, col * sh.noff, 0) - jnp.where(row == 3, 16384, 0)
    key = dot_tn(table.astype(BF16), weight.astype(F32).astype(BF16))
    return jnp.where((key >= 0.0) & (key < sh.noff), key, -1.0).astype(BF16)


def matches(keys, o):
    return jnp.where(keys == o, jnp.ones((), BF16), jnp.zeros((), BF16))


def tables_kernel(sh, mine_ref, counts_ref, target_ref, offset_ref, tmatrix_ref, lattice_ref, *refs):
    pairs_ref, turned_ref, flipped_ref, key_ref, lattice_vmem, flipped_vmem, sems, out_sems = refs
    groups = sh.noff // GROUP
    loads = [
        pltpu.make_async_copy(
            lattice_ref.at[pl.ds(g * GROUP, GROUP)], lattice_vmem.at[pl.ds(g * GROUP, GROUP)], sems.at[g]
        )
        for g in range(groups)
    ]
    for load in loads:
        load.start()
    count = counts_ref[mine_ref[0]]
    target = wrap(target_ref[...], count).astype(F32)
    offset = offset_ref[...].astype(F32)
    for n in range(sh.nl):
        key_ref[n] = slot_keys(sh, target[n : n + 1, :], offset[n : n + 1, :], None)
    for o in range(sh.noff):
        amount = matches(key_ref[0], jnp.asarray(o, BF16))
        for n in range(1, sh.nl):
            amount = amount + matches(key_ref[n], jnp.asarray(o, BF16))
        pairs_ref[o] = amount
    wide = identity(sh.width)
    turned_ref[...] = dot_nt(wide, tmatrix_ref[...]).astype(BF16)
    span = GROUP * sh.width
    stores = []
    for g in range(groups):
        loads[g].wait()
        some = lattice_vmem[g * GROUP : (g + 1) * GROUP].reshape(span, sh.width)
        flipped_vmem[g] = dot_nt(wide, some).astype(BF16)
        stores.append(pltpu.make_async_copy(flipped_vmem.at[g], flipped_ref.at[g], out_sems.at[g]))
        stores[g].start()
    for store in stores:
        store.wait()


def next_vector(step, current, olds, sums):
    if step == 0:
        return current / jnp.sqrt(sums[0])
    square = sums[step]
    kept = current
    for j in range(step):
        square = square - sums[j] * sums[j]
        kept = kept - sums[j] * olds[j]
    return -kept / jnp.sqrt(square)


def sort_slots(sh, recv_ref, count, key_ref, perm_ref, starts_ref):
    row8, lane = iota((8, LANES), 0), iota((LANES, LANES), 1)
    before = flag(iota((LANES, LANES), 1) < iota((LANES, LANES), 0))
    row, col = iota((8, LANES), 0), iota((8, LANES), 1)
    spread = jnp.where(row == 1, 1, jnp.where(row == 2, LANES, 0)).astype(F32).astype(BF16)
    tables, hits, places = [], [], []
    running = jnp.zeros((1, LANES), F32)
    for c in range(sh.chunks):
        table = jnp.zeros((8, LANES), F32)
        for s in range(c * sh.fold, (c + 1) * sh.fold):
            table = table + recv_ref[s].astype(F32)[sh.extra :]
        target = wrap(table[0:1].astype(jnp.int32), count).astype(F32)
        table = jnp.where(row8 == 0, target, jnp.where(row8 < 3, table, 0.0))
        tables.append(table)
        offset = dot_tn(table.astype(BF16), spread)
        hit = (offset == (lane + LANES).astype(F32)).astype(F32)
        hits.append(hit)
        places.append(dot(before, hit.astype(BF16)) + running)
        running = running + jnp.sum(hit, axis=0, keepdims=True)
    base = jnp.zeros((1, LANES), F32)
    high = jnp.floor(running * (1.0 / 64.0))
    after = flag(iota((LANES, LANES), 0) < iota((LANES, LANES), 1))
    both = jnp.where(row == 0, high, jnp.where(row == 1, running - 64.0 * high, 0.0))
    sums = dot(both.astype(BF16), after)
    base = 64.0 * sums[0:1] + sums[1:2]
    place_of = iota((LANES, sh.inbound), 1).astype(F32)
    for c in range(sh.chunks):
        place = jnp.sum(hits[c] * (places[c] + base + 1.0), axis=1, keepdims=True) - 1.0
        perm_ref[c * LANES : (c + 1) * LANES, :] = flag(place == place_of)
    table = dot(jnp.concatenate(tables, axis=1).astype(BF16), perm_ref[...])
    for c in range(sh.chunks):
        part = table[:, c * LANES : (c + 1) * LANES]
        key_ref[c * LANES : (c + 1) * LANES, :] = slot_keys(sh, part[0:1], part[1:2], 1.0 - part[2:3])
    fits = jnp.int32(1)
    edges = [jnp.sum(jnp.where(col[0:1] == g * GROUP, base, 0.0)).astype(jnp.int32) for g in range(sh.groups)]
    edges.append(jnp.sum(running).astype(jnp.int32))
    for g in range(sh.groups):
        begin = jnp.minimum(edges[g] // LANES, (sh.inbound - sh.window) // LANES)
        starts_ref[g] = begin
        fits = jnp.where(edges[g + 1] <= begin * LANES + sh.window, fits, 0)
    starts_ref[sh.groups] = fits


def step_kernel(sh, step, *refs):
    refs = list(refs)
    take = lambda n: [refs.pop(0) for _ in range(n)]
    mine_ref, counts_ref = take(2)
    starts_ref = take(1)[0] if step else None
    recv_ref, rank_ref, pairs_ref, turned_ref, flipped_ref, current_ref = take(6)
    olds = take(step)
    copies = take(step)
    key_ref, perm_ref = take(2) if step else (None, None)
    vector_out, image_out, sums_out, send_out = take(4)
    last = step == ITERS - 1
    copy_out = None if last else take(1)[0]
    if step == 0:
        key_ref, perm_ref, flipped_out, starts_ref = take(4)
    x_ref, sorted_ref, field_ref, *sems = refs
    groups = sh.noff // GROUP
    loads = []
    if step == 0:
        source, flipped_ref = flipped_ref, flipped_out
        loads = [pltpu.make_async_copy(source.at[g], flipped_ref.at[g], sems[0].at[g]) for g in range(groups)]
    for load in loads[:AHEAD]:
        load.start()
    mine = mine_ref[0]
    count = counts_ref[mine]
    extras = jnp.zeros((8, LANES), F32)
    for s in range(sh.tiles):
        extras = extras + recv_ref[s].astype(F32)[sh.extra :]
    sums = []
    for q in range(max(1, step + 1)):
        r = extras[4 + q : 5 + q]
        sums.append(r[:, 0:1] + r[:, 32:33] + r[:, 64:65])
    vector = next_vector(step, current_ref[...], [ref[...] for ref in olds], sums)
    vector_out[...] = vector
    own = vector.astype(BF16)
    if step == 0:
        sort_slots(sh, recv_ref, count, key_ref, perm_ref, starts_ref)
    lane_group = iota((1, LANES), 1) // sh.slots
    for c in range(sh.chunks):
        parts = []
        for f in range(sh.fold):
            part = recv_ref[c * sh.fold].astype(F32)[: sh.part]
            for m in range(1, sh.fold):
                other = recv_ref[c * sh.fold + m].astype(F32)[: sh.part]
                part = jnp.where(lane_group == (m + f) % sh.fold, other, part)
            if f:
                part = pltpu.roll(part, LANES - f * sh.slots, 1)
            parts.append(part)
        a = c * LANES
        column = next_vector(
            step, jnp.concatenate(parts, axis=0), [ref[:, a : a + LANES] for ref in copies], sums
        )
        if copy_out is not None:
            copy_out[:, a : a + LANES] = column
        x_ref[:, a : a + LANES] = column.astype(BF16)
    sorted_ref[...] = dot(x_ref[...], perm_ref[...]).astype(BF16)

    def gather(windowed):
        field = jnp.zeros((sh.width, sh.cap), F32)
        for g in range(groups):
            if windowed:
                at = pl.ds(pl.multiple_of(starts_ref[g] * LANES, LANES), sh.window)
            else:
                at = pl.ds(0, sh.inbound)
            counts_of = []
            for o in range(g * GROUP, (g + 1) * GROUP):
                counts_of.append(
                    jnp.concatenate([pairs_ref[o], matches(key_ref[at, :], jnp.asarray(o, BF16))], axis=0)
                )
            columns = jnp.concatenate([own, sorted_ref[:, at]], axis=1)
            summed = dot(columns, jnp.concatenate(counts_of, axis=1)).astype(BF16)
            stack = jnp.concatenate([summed[:, q * sh.cap : (q + 1) * sh.cap] for q in range(GROUP)], axis=0)
            if loads:
                loads[g].wait()
                if g + AHEAD < groups:
                    loads[g + AHEAD].start()
            field = field + dot(flipped_ref[g], stack)
        field_ref[...] = field

    fits = starts_ref[sh.groups]
    pl.when(fits == 1)(functools.partial(gather, True))
    pl.when(fits != 1)(functools.partial(gather, False))
    field = field_ref[...]
    live = (iota((1, sh.cap), 1) < count).astype(F32)
    image = live * dot(turned_ref[...], field.astype(BF16))
    image_out[...] = image
    out = [total(ref[...] * image) for ref in olds] + [total(vector * image), total(image * image)]
    row8 = iota((8, LANES), 0)
    seen = jnp.zeros((8, LANES), F32)
    for q, value in enumerate(sums):
        seen = jnp.where(row8 == q, value, seen)
    sums_out[...] = seen
    if last:
        col = iota((1, LANES), 1)
        tile = jnp.zeros((1, LANES), F32)
        for q, value in enumerate(out):
            tile = jnp.where(col == q, value, tile)
        for d in range(sh.tiles):
            send_out[d] = tile
    else:
        tile = sum_rows(out)
        pack(sh, mine, image.astype(BF16), rank_ref, send_out, lambda d, picked: tile)


def last_kernel(sh, recv_ref, *refs):
    seen = refs[:ITERS]
    vectors = refs[ITERS : 2 * ITERS]
    image_ref, basis_ref, hess_ref = refs[2 * ITERS :]
    final = jnp.zeros((1, LANES), F32)
    for s in range(sh.tiles):
        final = final + recv_ref[s]
    sums = [final[:, q : q + 1] for q in range(ITERS + 1)]
    tables = [[ref[q : q + 1, 0:1] for q in range(ITERS)] for ref in seen[1:]] + [sums]
    row = iota((ITERS + 1, ITERS), 0)
    col = iota((ITERS + 1, ITERS), 1)
    hess = jnp.zeros((ITERS + 1, ITERS), F32)
    for k in range(ITERS):
        square = tables[k][k + 1]
        for j in range(k + 1):
            product = tables[k][j]
            square = square - product * product
            hess = jnp.where((row == j) & (col == k), (1.0 if j == k else 0.0) - product, hess)
        hess = jnp.where((row == k + 1) & (col == k), jnp.sqrt(square), hess)
    hess_ref[...] = hess
    olds = [ref[...] for ref in vectors]
    for j in range(ITERS):
        basis_ref[j] = olds[j]
    basis_ref[ITERS] = next_vector(ITERS, image_ref[...], olds, sums)


def call(kernel, name, outs, args, smem=0, plain=False, hbm=(), out_hbm=(), out_plain=(), out_smem=(), scratch=()):
    specs, placed = [], []
    for i, arg in enumerate(args):
        space = pltpu.SMEM if i < smem else pl.ANY if i in hbm else pltpu.VMEM
        specs.append(pl.BlockSpec(memory_space=space))
        held = pltpu.HBM if i < smem or plain or i in hbm else pltpu.VMEM
        placed.append(pltpu.with_memory_space_constraint(arg, held))
    return pl.pallas_call(
        kernel,
        name=name,
        out_shape=[
            pltpu.HBM(shape, dtype) if i in (*out_plain, *out_hbm, *out_smem) else pltpu.VMEM(shape, dtype)
            for i, (shape, dtype) in enumerate(outs)
        ],
        in_specs=specs,
        out_specs=[
            pl.BlockSpec(
                memory_space=pl.ANY if i in out_hbm else pltpu.SMEM if i in out_smem else pltpu.VMEM
            )
            for i in range(len(outs))
        ],
        scratch_shapes=list(scratch),
        compiler_params=pltpu.CompilerParams(vmem_limit_bytes=VMEM_LIMIT),
    )(*placed)


def per_device(
    rhs,
    counts,
    local_target,
    local_offset,
    remote_tile,
    remote_target,
    remote_offset,
    lattice,
    tmatrix,
):
    tiles = lax.axis_size("tile")
    cap, width = rhs.shape
    noff = lattice.shape[0]
    sh = Shape(tiles, cap, width, local_target.shape[1], remote_tile.shape[1], noff)
    mine = lax.axis_index("tile").astype(jnp.int32).reshape(1)
    exchange = functools.partial(
        lax.all_to_all, axis_name="tile", split_axis=0, concat_axis=0, tiled=True
    )
    own = ((width, cap), F32)
    block = ((tiles, sh.rows, LANES), BF16)
    groups = noff // GROUP
    lattice_shape = (groups, width, GROUP * width)
    start, rank, send = call(
        functools.partial(first_kernel, sh),
        "first",
        [own, ((tiles, cap), jnp.int32), block],
        [mine, counts, rhs.T, remote_tile.T, remote_target.T, remote_offset.T],
        smem=2,
        plain=True,
        scratch=[pltpu.VMEM((3, tiles, cap), F32)],
    )
    recv = exchange(send)
    pairs, turned, flipped = call(
        functools.partial(tables_kernel, sh),
        "tables",
        [((noff, cap, cap), BF16), ((width, width), BF16), (lattice_shape, BF16)],
        [mine, counts, local_target.T, local_offset.T, tmatrix, lattice],
        smem=2,
        plain=True,
        hbm=(5,),
        out_hbm=(2,),
        scratch=[
            pltpu.VMEM((sh.nl, cap, cap), BF16),
            pltpu.VMEM((noff, width, width), BF16),
            pltpu.VMEM(lattice_shape, BF16),
            pltpu.SemaphoreType.DMA((groups,)),
            pltpu.SemaphoreType.DMA((groups,)),
        ],
    )
    current, olds, copies, keys, seen, starts = start, [], [], [], [], []
    for step in range(ITERS):
        last = step == ITERS - 1
        outs = [own, own, ((8, LANES), F32)]
        outs.append(((tiles, 1, LANES), F32) if last else block)
        if not last:
            outs.append(((width, sh.inbound), F32))
        if step == 0:
            outs.append(((sh.inbound, LANES), BF16))
            outs.append(((sh.inbound, sh.inbound), BF16))
            outs.append((lattice_shape, BF16))
            outs.append(((groups + 1,), jnp.int32))
        scalars = [mine, counts, *starts]
        result = call(
            functools.partial(step_kernel, sh, step),
            f"step{step}",
            outs,
            [*scalars, recv, rank, pairs, turned, flipped, current, *olds, *copies, *keys],
            smem=len(scalars),
            hbm=() if step else (6,),
            out_smem=() if step else (8,),
            scratch=[
                pltpu.VMEM((width, sh.inbound), BF16),
                pltpu.VMEM((width, sh.inbound), BF16),
                pltpu.VMEM((width, cap), F32),
            ]
            + ([] if step else [pltpu.SemaphoreType.DMA((groups,))]),
        )
        vector, current, sums, send = result[:4]
        olds.append(vector)
        seen.append(sums)
        if not last:
            copies.append(result[4])
        if step == 0:
            keys, flipped, starts = result[5:7], result[7], [result[8]]
        recv = exchange(send)
    basis, hess = call(
        functools.partial(last_kernel, sh),
        "last",
        [((ITERS + 1, width, cap), F32), ((ITERS + 1, ITERS), F32)],
        [recv, *seen, *olds, current],
        out_plain=(0, 1),
    )
    return jnp.transpose(basis, (0, 2, 1)), hess


def solution(mesh):
    placed = (
        P(("groups", "tile"), None),
        P("groups"),
        P(("groups", "tile"), None),
        P(("groups", "tile"), None),
        P(("groups", "tile"), None),
        P(("groups", "tile"), None),
        P(("groups", "tile"), None),
        P(),
        P(),
    )
    return jax.shard_map(
        per_device,
        mesh=mesh,
        in_specs=placed,
        out_specs=(P(None, ("groups", "tile"), None), P("groups", None)),
        check_vma=False,
    )
```

```python
import functools

import jax
import jax.numpy as jnp
from jax import lax
from jax.experimental import pallas as pl
from jax.experimental.pallas import tpu as pltpu
from jax.sharding import PartitionSpec as P

ITERS = 3
LANES = 128
GROUP = 8
AHEAD = 2
BLOCKS = 2
F32 = jnp.float32
BF16 = jnp.bfloat16
VMEM_LIMIT = 28 * 1024 * 1024


def iota(shape, dim):
    return lax.broadcasted_iota(jnp.int32, shape, dim)


def dot(a, b):
    return lax.dot_general(a, b, (((1,), (0,)), ((), ())), preferred_element_type=F32)


def dot_nt(a, b):
    return lax.dot_general(a, b, (((1,), (1,)), ((), ())), preferred_element_type=F32)


def dot_tn(a, b):
    return lax.dot_general(a, b, (((0,), (0,)), ((), ())), preferred_element_type=F32)


def flag(mask):
    return mask.astype(F32).astype(BF16)


def identity(size):
    return flag(iota((size, size), 0) == iota((size, size), 1))


def total(values):
    return jnp.sum(jnp.sum(values, axis=0, keepdims=True), axis=1, keepdims=True)


def pieces(value):
    first = value.astype(BF16).astype(F32)
    rest = value - first
    second = rest.astype(BF16).astype(F32)
    return first, second, rest - second


def wrap(target, count):
    for _ in range(3):
        target = jnp.where(target >= count, target - count, target)
    return target


def each(amount, body):
    if amount <= 16:
        for i in range(amount):
            body(i)
    else:
        lax.fori_loop(0, amount, lambda i, carry: (body(i), carry)[1], 0)


class Shape:
    def __init__(self, tiles, cap, width, nl, nr, noff):
        self.tiles, self.cap, self.width, self.nl, self.nr, self.noff = tiles, cap, width, nl, nr, noff
        self.send_cap = max(2, 2 * cap * nr // tiles)
        self.slots = max(16, self.send_cap)
        self.fold = LANES // self.slots
        self.part = width // self.fold
        self.extra = -(-self.part // 8) * 8
        self.rows = self.extra + 8
        self.chunks = tiles // self.fold
        self.inbound = self.chunks * LANES
        self.sources = cap + self.inbound


def pack(sh, mine, values, rank_ref, out_ref, extra):
    parts = [values[f * sh.part : (f + 1) * sh.part] for f in range(sh.fold)]
    wide = jnp.concatenate(parts, axis=1)
    lane = iota((LANES, sh.cap), 0)
    shifts = [lax.rem(mine + f, sh.fold) * sh.slots for f in range(sh.fold)]

    def body(e):
        some = []
        for d in range(BLOCKS):
            rank = rank_ref[pl.ds(e * BLOCKS + d, 1), :]
            some.append([flag(rank + shift == lane) for shift in shifts])
        picked = jnp.concatenate([jnp.concatenate(one, axis=1) for one in some], axis=0)
        blocks = dot_nt(wide, picked)
        for d in range(BLOCKS):
            block = [blocks[:, d * LANES : (d + 1) * LANES]]
            if sh.extra > sh.part:
                block.append(jnp.zeros((sh.extra - sh.part, LANES), F32))
            block.append(extra(e * BLOCKS + d, some[d][0]))
            out_ref[e * BLOCKS + d] = jnp.concatenate(block, axis=0).astype(BF16)

    each(sh.tiles // BLOCKS, body)


def sum_rows(sums):
    row, col = iota((8, LANES), 0), iota((8, LANES), 1)
    tile = jnp.zeros((8, LANES), F32)
    for q, value in enumerate(sums):
        first, second, third = pieces(value)
        spread = jnp.where(col < 32, first, jnp.where(col < 64, second, third))
        tile = jnp.where(row == 4 + q, spread, tile)
    return tile


def first_kernel(sh, mine_ref, counts_ref, rhs_ref, tile_ref, target_ref, offset_ref,
                 start_ref, rank_ref, out_ref, code_ref):
    mine = mine_ref[0]
    count = counts_ref[mine]
    start = rhs_ref[...] * (iota((1, sh.cap), 1) < count).astype(F32)
    start_ref[...] = start
    tile = tile_ref[...]
    target = target_ref[...].astype(F32)
    offset = offset_ref[...].astype(F32)
    which = iota((sh.tiles, sh.cap), 0)
    named = jnp.zeros((sh.tiles, sh.cap), F32)
    targets = jnp.zeros((sh.tiles, sh.cap), F32)
    offsets = jnp.zeros((sh.tiles, sh.cap), F32)
    for r in range(sh.nr):
        hit = tile[r : r + 1, :] == which
        named = jnp.where(hit, 1.0, named)
        targets = jnp.where(hit, target[r : r + 1, :], targets)
        offsets = jnp.where(hit, offset[r : r + 1, :], offsets)
    before = flag(iota((sh.cap, sh.cap), 0) < iota((sh.cap, sh.cap), 1))
    rank = dot(named.astype(BF16), before).astype(jnp.int32)
    rank_ref[...] = jnp.where(named > 0.0, rank, -2 * LANES)
    code_ref[0] = targets
    code_ref[1] = offsets
    code_ref[2] = named
    sums = sum_rows([total(start * start)])
    row = iota((8, LANES), 0)

    def extra(d, picked):
        table = jnp.zeros((8, sh.cap), F32)
        for q in range(3):
            table = jnp.where(row == q, code_ref[q, pl.ds(d, 1), :], table)
        return dot_nt(table.astype(BF16), picked) + sums

    pack(sh, mine, start.astype(BF16), rank_ref, out_ref, extra)


def slot_keys(sh, target, offset, empty):
    rows = iota((16, target.shape[1]), 0)
    table = jnp.where(rows == 0, target, 0.0)
    table = jnp.where(rows == 1, offset, table)
    table = jnp.where(rows == 2, 1.0, table)
    if empty is not None:
        table = jnp.where(rows == 3, empty, table)
    row, col = iota((16, sh.cap), 0), iota((16, sh.cap), 1)
    weight = jnp.where(row == 0, sh.noff, 0) + jnp.where(row == 1, 1, 0)
    weight = weight - jnp.where(row == 2, col * sh.noff, 0) - jnp.where(row == 3, 16384, 0)
    key = dot_tn(table.astype(BF16), weight.astype(F32).astype(BF16))
    return jnp.where((key >= 0.0) & (key < sh.noff), key, -1.0).astype(BF16)


def matches(keys, o):
    return jnp.where(keys == o, jnp.ones((), BF16), jnp.zeros((), BF16))


def tables_kernel(sh, mine_ref, counts_ref, target_ref, offset_ref, tmatrix_ref, lattice_ref, *refs):
    pairs_ref, turned_ref, flipped_ref, key_ref, lattice_vmem, flipped_vmem, sems, out_sems = refs
    groups = sh.noff // GROUP
    loads = [
        pltpu.make_async_copy(
            lattice_ref.at[pl.ds(g * GROUP, GROUP)], lattice_vmem.at[pl.ds(g * GROUP, GROUP)], sems.at[g]
        )
        for g in range(groups)
    ]
    for load in loads:
        load.start()
    count = counts_ref[mine_ref[0]]
    target = wrap(target_ref[...], count).astype(F32)
    offset = offset_ref[...].astype(F32)
    for n in range(sh.nl):
        key_ref[n] = slot_keys(sh, target[n : n + 1, :], offset[n : n + 1, :], None)
    for o in range(sh.noff):
        amount = matches(key_ref[0], jnp.asarray(o, BF16))
        for n in range(1, sh.nl):
            amount = amount + matches(key_ref[n], jnp.asarray(o, BF16))
        pairs_ref[o] = amount
    wide = identity(sh.width)
    turned_ref[...] = dot_nt(wide, tmatrix_ref[...]).astype(BF16)
    span = GROUP * sh.width
    stores = []
    for g in range(groups):
        loads[g].wait()
        some = lattice_vmem[g * GROUP : (g + 1) * GROUP].reshape(span, sh.width)
        flipped_vmem[g] = dot_nt(wide, some).astype(BF16)
        stores.append(pltpu.make_async_copy(flipped_vmem.at[g], flipped_ref.at[g], out_sems.at[g]))
        stores[g].start()
    for store in stores:
        store.wait()


def next_vector(step, current, olds, sums):
    if step == 0:
        return current / jnp.sqrt(sums[0])
    square = sums[step]
    kept = current
    for j in range(step):
        square = square - sums[j] * sums[j]
        kept = kept - sums[j] * olds[j]
    return -kept / jnp.sqrt(square)


def step_kernel(sh, step, *refs):
    refs = list(refs)
    take = lambda n: [refs.pop(0) for _ in range(n)]
    mine_ref, counts_ref, recv_ref, rank_ref, pairs_ref, turned_ref = take(6)
    flipped_ref, current_ref = take(2)
    olds = take(step)
    copies = take(step)
    key_in = take(1 if step else 0)
    vector_out, image_out, sums_out, send_out = take(4)
    last = step == ITERS - 1
    copy_out = None if last else take(1)[0]
    key_out = take(0 if step else 1)
    flipped_out = take(0 if step else 1)
    x_ref, *sems = refs
    groups = sh.noff // GROUP
    loads = []
    if step == 0:
        source, flipped_ref = flipped_ref, flipped_out[0]
        loads = [pltpu.make_async_copy(source.at[g], flipped_ref.at[g], sems[0].at[g]) for g in range(groups)]
    for load in loads[:AHEAD]:
        load.start()
    mine = mine_ref[0]
    count = counts_ref[mine]
    extras = jnp.zeros((8, LANES), F32)
    for s in range(sh.tiles):
        extras = extras + recv_ref[s].astype(F32)[sh.extra :]
    sums = []
    for q in range(max(1, step + 1)):
        r = extras[4 + q : 5 + q]
        sums.append(r[:, 0:1] + r[:, 32:33] + r[:, 64:65])
    vector = next_vector(step, current_ref[...], [ref[...] for ref in olds], sums)
    vector_out[...] = vector
    x_ref[:, 0 : sh.cap] = vector.astype(BF16)
    if step == 0:
        key_ref = key_out[0]
        for c in range(sh.chunks):
            table = jnp.zeros((8, LANES), F32)
            for s in range(c * sh.fold, (c + 1) * sh.fold):
                table = table + recv_ref[s].astype(F32)[sh.extra :]
            target = wrap(table[0:1].astype(jnp.int32), count).astype(F32)
            key_ref[c * LANES : (c + 1) * LANES, :] = slot_keys(sh, target, table[1:2], 1.0 - table[2:3])
    else:
        key_ref = key_in[0]
    lane_group = iota((1, LANES), 1) // sh.slots
    for c in range(sh.chunks):
        parts = []
        for f in range(sh.fold):
            part = recv_ref[c * sh.fold].astype(F32)[: sh.part]
            for m in range(1, sh.fold):
                other = recv_ref[c * sh.fold + m].astype(F32)[: sh.part]
                part = jnp.where(lane_group == (m + f) % sh.fold, other, part)
            if f:
                part = pltpu.roll(part, LANES - f * sh.slots, 1)
            parts.append(part)
        a = c * LANES
        column = next_vector(
            step, jnp.concatenate(parts, axis=0), [ref[:, a : a + LANES] for ref in copies], sums
        )
        if copy_out is not None:
            copy_out[:, a : a + LANES] = column
        x_ref[:, sh.cap + a : sh.cap + a + LANES] = column.astype(BF16)
    field = jnp.zeros((sh.width, sh.cap), F32)
    for g in range(groups):
        counts_of = []
        for o in range(g * GROUP, (g + 1) * GROUP):
            hits = matches(key_ref[...], jnp.asarray(o, BF16))
            counts_of.append(jnp.concatenate([pairs_ref[o], hits], axis=0))
        summed = dot(x_ref[...], jnp.concatenate(counts_of, axis=1)).astype(BF16)
        stack = jnp.concatenate([summed[:, q * sh.cap : (q + 1) * sh.cap] for q in range(GROUP)], axis=0)
        if loads:
            loads[g].wait()
            if g + AHEAD < groups:
                loads[g + AHEAD].start()
        field = field + dot(flipped_ref[g], stack)
    live = (iota((1, sh.cap), 1) < count).astype(F32)
    image = live * dot(turned_ref[...], field.astype(BF16))
    image_out[...] = image
    out = [total(ref[...] * image) for ref in olds] + [total(vector * image), total(image * image)]
    row8 = iota((8, LANES), 0)
    seen = jnp.zeros((8, LANES), F32)
    for q, value in enumerate(sums):
        seen = jnp.where(row8 == q, value, seen)
    sums_out[...] = seen
    if last:
        col = iota((1, LANES), 1)
        tile = jnp.zeros((1, LANES), F32)
        for q, value in enumerate(out):
            tile = jnp.where(col == q, value, tile)
        for d in range(sh.tiles):
            send_out[d] = tile
    else:
        tile = sum_rows(out)
        pack(sh, mine, image.astype(BF16), rank_ref, send_out, lambda d, picked: tile)


def last_kernel(sh, recv_ref, *refs):
    seen = refs[:ITERS]
    vectors = refs[ITERS : 2 * ITERS]
    image_ref, basis_ref, hess_ref = refs[2 * ITERS :]
    final = jnp.zeros((1, LANES), F32)
    for s in range(sh.tiles):
        final = final + recv_ref[s]
    sums = [final[:, q : q + 1] for q in range(ITERS + 1)]
    tables = [[ref[q : q + 1, 0:1] for q in range(ITERS)] for ref in seen[1:]] + [sums]
    row = iota((ITERS + 1, ITERS), 0)
    col = iota((ITERS + 1, ITERS), 1)
    hess = jnp.zeros((ITERS + 1, ITERS), F32)
    for k in range(ITERS):
        square = tables[k][k + 1]
        for j in range(k + 1):
            product = tables[k][j]
            square = square - product * product
            hess = jnp.where((row == j) & (col == k), (1.0 if j == k else 0.0) - product, hess)
        hess = jnp.where((row == k + 1) & (col == k), jnp.sqrt(square), hess)
    hess_ref[...] = hess
    olds = [ref[...] for ref in vectors]
    for j in range(ITERS):
        basis_ref[j] = olds[j]
    basis_ref[ITERS] = next_vector(ITERS, image_ref[...], olds, sums)


def call(kernel, name, outs, args, smem=0, plain=False, hbm=(), out_hbm=(), out_plain=(), scratch=()):
    specs, placed = [], []
    for i, arg in enumerate(args):
        space = pltpu.SMEM if i < smem else pl.ANY if i in hbm else pltpu.VMEM
        specs.append(pl.BlockSpec(memory_space=space))
        held = pltpu.HBM if i < smem or plain or i in hbm else pltpu.VMEM
        placed.append(pltpu.with_memory_space_constraint(arg, held))
    return pl.pallas_call(
        kernel,
        name=name,
        out_shape=[
            pltpu.HBM(shape, dtype) if i in out_plain or i in out_hbm else pltpu.VMEM(shape, dtype)
            for i, (shape, dtype) in enumerate(outs)
        ],
        in_specs=specs,
        out_specs=[
            pl.BlockSpec(memory_space=pl.ANY if i in out_hbm else pltpu.VMEM) for i in range(len(outs))
        ],
        scratch_shapes=list(scratch),
        compiler_params=pltpu.CompilerParams(vmem_limit_bytes=VMEM_LIMIT),
    )(*placed)


def per_device(
    rhs,
    counts,
    local_target,
    local_offset,
    remote_tile,
    remote_target,
    remote_offset,
    lattice,
    tmatrix,
):
    tiles = lax.axis_size("tile")
    cap, width = rhs.shape
    noff = lattice.shape[0]
    sh = Shape(tiles, cap, width, local_target.shape[1], remote_tile.shape[1], noff)
    mine = lax.axis_index("tile").astype(jnp.int32).reshape(1)
    exchange = functools.partial(
        lax.all_to_all, axis_name="tile", split_axis=0, concat_axis=0, tiled=True
    )
    own = ((width, cap), F32)
    block = ((tiles, sh.rows, LANES), BF16)
    groups = noff // GROUP
    lattice_shape = (groups, width, GROUP * width)
    start, rank, send = call(
        functools.partial(first_kernel, sh),
        "first",
        [own, ((tiles, cap), jnp.int32), block],
        [mine, counts, rhs.T, remote_tile.T, remote_target.T, remote_offset.T],
        smem=2,
        plain=True,
        scratch=[pltpu.VMEM((3, tiles, cap), F32)],
    )
    recv = exchange(send)
    pairs, turned, flipped = call(
        functools.partial(tables_kernel, sh),
        "tables",
        [((noff, cap, cap), BF16), ((width, width), BF16), (lattice_shape, BF16)],
        [mine, counts, local_target.T, local_offset.T, tmatrix, lattice],
        smem=2,
        plain=True,
        hbm=(5,),
        out_hbm=(2,),
        scratch=[
            pltpu.VMEM((sh.nl, cap, cap), BF16),
            pltpu.VMEM((noff, width, width), BF16),
            pltpu.VMEM(lattice_shape, BF16),
            pltpu.SemaphoreType.DMA((groups,)),
            pltpu.SemaphoreType.DMA((groups,)),
        ],
    )
    current, olds, copies, keys, seen = start, [], [], [], []
    for step in range(ITERS):
        last = step == ITERS - 1
        outs = [own, own, ((8, LANES), F32)]
        outs.append(((tiles, 1, LANES), F32) if last else block)
        if not last:
            outs.append(((width, sh.inbound), F32))
        if step == 0:
            outs.append(((sh.inbound, LANES), BF16))
            outs.append((lattice_shape, BF16))
        result = call(
            functools.partial(step_kernel, sh, step),
            f"step{step}",
            outs,
            [mine, counts, recv, rank, pairs, turned, flipped, current, *olds, *copies, *keys],
            smem=2,
            hbm=() if step else (6,),
            scratch=[pltpu.VMEM((width, sh.sources), BF16)]
            + ([] if step else [pltpu.SemaphoreType.DMA((groups,))]),
        )
        vector, current, sums, send = result[:4]
        olds.append(vector)
        seen.append(sums)
        if not last:
            copies.append(result[4])
        if step == 0:
            keys, flipped = [result[5]], result[6]
        recv = exchange(send)
    basis, hess = call(
        functools.partial(last_kernel, sh),
        "last",
        [((ITERS + 1, width, cap), F32), ((ITERS + 1, ITERS), F32)],
        [recv, *seen, *olds, current],
        out_plain=(0, 1),
    )
    return jnp.transpose(basis, (0, 2, 1)), hess


def solution(mesh):
    placed = (
        P(("groups", "tile"), None),
        P("groups"),
        P(("groups", "tile"), None),
        P(("groups", "tile"), None),
        P(("groups", "tile"), None),
        P(("groups", "tile"), None),
        P(("groups", "tile"), None),
        P(),
        P(),
    )
    return jax.shard_map(
        per_device,
        mesh=mesh,
        in_specs=placed,
        out_specs=(P(None, ("groups", "tile"), None), P("groups", None)),
        check_vma=False,
    )
```
